32 devices in a mesh: beam: 4 (over x, core), depth: 8 (over z, y).
Axes of the slice: x: 2, y: 2, z: 4, core: 2. Of those that a mesh axis runs over, the one named last changes fastest.
Arguments:
- concentration: float32 [128, 1024, 256], P('beam', 'depth'), may hold values from 0.25 to 2.5
- entry_intensity: float32 [1024, 256], P('depth'), may hold values from 0.25 to 1.75
- absorb: float32 [256], replicated, may hold values from 0.0015625 to 0.01953125
- blur_taps: float32 [5], replicated, may hold values from 0.1 to 1
- measured: float32 [128, 256], P('beam'), may hold values from -6 to 6
Outputs:
- descent: float32 [128, 1024, 256], P('beam', 'depth')
- residual: float32 [128, 256], P('beam', 'depth')
The draws below stay inside these ranges and needn't reach their ends.
All inputs are finite; a program needn't handle non-finite values.
Results may differ from the reference program's by a relative error of at most 0.000058.
Values sent between devices are 32-bit elements; how exact they have to be, the bound alone decides.
A program may use at most 64 MiB of HBM per device.

```python
import math
import jax
import jax.numpy as jnp
from jax import lax

CD = 128
H = 256
TAPS = 5
NB = 128
ND = 1024
N_DEPTH = 8


def shard_levels(key, shape, shards, low, high):
    def one(dim, blocks):
        heights = jax.random.uniform(jax.random.fold_in(jax.random.fold_in(key, 6), dim), (blocks,), jnp.float32, low / len(shards), high / len(shards))
        return jnp.repeat(jnp.exp(heights), shape[dim] // blocks).reshape((-1,) + (1,) * (len(shape) - dim - 1))

    gain = one(*shards[0])
    for cut in shards[1:]:
        gain = gain * one(*cut)
    return gain


def bell_draw(own_key, extent, deviation, most, cuts=(), held_as=jnp.bfloat16):
    values = jax.random.normal(own_key, extent, jnp.float32) * deviation
    if len(cuts) > 0:
        values = shard_levels(own_key, extent, cuts, -0.22, 0.18) * values
    return jnp.clip(values, min=-most, max=most).astype(held_as)


def setup_inputs(seed: int = 0) -> dict:
    arg_keys = jax.random.split(jax.random.key(seed), 6)
    concentration = jnp.clip(jnp.exp(math.log(2.5) - 2.3025851 * jax.random.uniform(arg_keys[0], (NB, ND, H), jnp.float32) ** shard_levels(arg_keys[0], (NB, ND, H), ((0, 4), (1, 8)), -0.2, 0.2)), 0.25, 2.5)
    entry_intensity = jnp.clip(1.0 + 0.15 * jax.random.normal(arg_keys[1], (ND, H), jnp.float32), 0.25, 1.75)
    absorb = jnp.clip(jnp.exp(jax.random.uniform(arg_keys[2], (H,), jnp.float32, math.log(0.0015625), math.log(0.01953125))), 0.0015625, 0.01953125)
    blur_taps = jnp.clip(jnp.exp(jax.random.uniform(arg_keys[3], (TAPS,), jnp.float32, math.log(0.1), math.log(1.0))), 0.1, 1.0)
    measured = bell_draw(arg_keys[4], (NB, H), 1.0, 6.0, ((0, 4),), jnp.float32)
    return {"concentration": concentration, "entry_intensity": entry_intensity, "absorb": absorb, "blur_taps": blur_taps, "measured": measured}


def blur_rows(padded, blur_taps, width):
    total = blur_taps[0] * padded[:, 0:width]
    for k in range(1, 5):
        total = total + blur_taps[k] * padded[:, k:k + width]
    return total


def adjoint_rows(padded, blur_taps, width):
    total = blur_taps[0] * padded[:, 4:4 + width]
    for k in range(1, 5):
        total = total + blur_taps[k] * padded[:, 4 - k:4 - k + width]
    return total


def reference(concentration, entry_intensity, absorb, blur_taps, measured):
    starts = jnp.arange(N_DEPTH, dtype=jnp.int32) * CD

    def lit_block(start):
        block = lax.dynamic_slice_in_dim(concentration, start, CD, 1)
        light = lax.dynamic_slice_in_dim(entry_intensity, start, CD, 0)
        inclusive = jnp.cumsum(block, axis=0)
        prior = jnp.concatenate([jnp.zeros((1, CD, H), jnp.float32), inclusive[:-1]], axis=0)
        lit = light[None] * jnp.exp(-absorb * prior)
        return block, lit

    def emit(start):
        block, lit = lit_block(start)
        return jnp.sum(lit * block, axis=1)

    image = jnp.sum(lax.map(emit, starts), axis=0) / ND
    padded = jnp.pad(image, ((0, 0), (2, 2)))
    residual = blur_rows(padded, blur_taps, H) - measured
    back = adjoint_rows(jnp.pad(residual, ((0, 0), (2, 2))), blur_taps, H)

    def gradient(start):
        block, lit = lit_block(start)
        q = back[:, None, :] * lit
        weighted = q * block
        inclusive = jnp.cumsum(weighted[::-1], axis=0)[::-1]
        later = jnp.concatenate([inclusive[1:], jnp.zeros((1, CD, H), jnp.float32)], axis=0)
        return absorb * later - q

    blocks = lax.map(gradient, starts)
    descent = jnp.transpose(blocks, (1, 0, 2, 3)).reshape(NB, ND, H)
    return descent, residual
```

```python
import functools

import jax
import jax.numpy as jnp
from jax import lax
from jax.experimental import pallas as pl
from jax.experimental.pallas import tpu as pltpu
from jax.sharding import PartitionSpec as P

MESH = pl.DeviceIdType.MESH
ROWS, LANES = 8, 128
CHUNKS = 4


def blur(x, taps, sign):
    width = x.shape[1]
    lane = lax.broadcasted_iota(jnp.int32, x.shape, 1)
    total = jnp.zeros_like(x)
    for k in range(5):
        step = sign * (k - 2)
        moved = x if step == 0 else pltpu.roll(x, (-step) % width, 1)
        inside = (lane + step >= 0) & (lane + step < width)
        total = total + taps[k] * jnp.where(inside, moved, 0.0)
    return total


def exchange_kernel(
    nb, nd, c_hbm, entry, absorb, taps_ref, measured,
    light_out, back_out, after_out, res_out,
    w, tot, pbuf, ps, qbuf, fs, fbuf, before, img, rs, ag,
    load_sem, a_send, a_recv, b_send, b_recv, f_send, f_recv,
    rs_send, rs_recv, ag_send, ag_recv,
):
    cells, depth, height = w.shape
    half = depth // 2
    pairs = nb // 2
    bi = lax.axis_index("beam")
    di = lax.axis_index("depth")
    core = lax.rem(bi, 2)
    pair = bi // 2
    partner = bi + 1 - 2 * core
    tiles = depth // ROWS
    lane_blocks = height // LANES
    pieces = (cells // ROWS) * lane_blocks
    owners = min(nd, pieces)
    per = pieces // owners

    step = depth // CHUNKS
    loads = []
    for k in range(CHUNKS):
        part = pl.ds(k * step, step)
        copy = pltpu.make_async_copy(c_hbm.at[:, part, :], w.at[:, part, :], load_sem.at[k])
        copy.start()
        loads.append(copy)

    barrier = pltpu.get_barrier_semaphore()
    for k in range(1, nb):
        pl.semaphore_signal(
            barrier, inc=1, device_id={"beam": lax.rem(bi + k, nb)}, device_id_type=MESH
        )
    for k in range(1, nd):
        pl.semaphore_signal(
            barrier, inc=1, device_id={"depth": lax.rem(di + k, nd)}, device_id_type=MESH
        )

    def totals(i, carry):
        rows = pl.ds(pl.multiple_of(i * ROWS, ROWS), ROWS)
        parts = [w[b, rows, :] for b in range(4)]
        for b in range(4, cells):
            parts[b % 4] = parts[b % 4] + w[b, rows, :]
        tot[0, rows, :] = (parts[0] + parts[1]) + (parts[2] + parts[3])
        return carry

    for k in range(CHUNKS):
        loads[k].wait()
        lax.fori_loop(k * step // ROWS, (k + 1) * step // ROWS, totals, 0)

    pl.semaphore_wait(barrier, nb - 1 + nd - 1)

    own_rows = pl.ds(pl.multiple_of(core * half, ROWS), half)
    other_rows = pl.ds(pl.multiple_of((1 - core) * half, ROWS), half)

    def to_partner(ph, slot):
        return pltpu.make_async_remote_copy(
            src_ref=tot.at[ph, other_rows if slot == 0 else own_rows, :],
            dst_ref=pbuf.at[ph, slot],
            send_sem=a_send.at[ph, slot],
            recv_sem=a_recv.at[ph, slot],
            device_id={"beam": partner},
            device_id_type=MESH,
        )

    def to_pair(ph, target):
        return pltpu.make_async_remote_copy(
            src_ref=ps.at[ph],
            dst_ref=qbuf.at[ph, pair],
            send_sem=b_send.at[ph, target],
            recv_sem=b_recv.at[ph, pair],
            device_id={"beam": 2 * target + core},
            device_id_type=MESH,
        )

    def from_pair(ph, source):
        return pltpu.make_async_remote_copy(
            src_ref=ps.at[ph],
            dst_ref=qbuf.at[ph, source],
            send_sem=b_send.at[ph, source],
            recv_sem=b_recv.at[ph, source],
            device_id={"beam": 2 * source + core},
            device_id_type=MESH,
        )

    def forward(ph):
        return pltpu.make_async_remote_copy(
            src_ref=fs.at[ph],
            dst_ref=fbuf.at[ph],
            send_sem=f_send.at[ph],
            recv_sem=f_recv.at[ph],
            device_id={"beam": partner},
            device_id_type=MESH,
        )

    def downstream(ph, other):
        return other > pair if ph == 0 else other < pair

    def upstream(ph, other):
        return other < pair if ph == 0 else other > pair

    def exchange_begin(ph):
        to_partner(ph, 0).start()
        to_partner(ph, 1).start()
        to_partner(ph, 0).wait_recv()
        if pairs > 1:
            ps[ph] = tot[ph, own_rows, :] + pbuf[ph, 0]
            for target in range(pairs):
                @pl.when(downstream(ph, target))
                def _():
                    to_pair(ph, target).start()

    def exchange_end(ph, result):
        to_partner(ph, 1).wait_recv()
        takes = core == (1 if ph == 0 else 0)

        @pl.when(takes)
        def _():
            result[own_rows, :] = pbuf[ph, 0]
            result[other_rows, :] = pbuf[ph, 1]

        @pl.when(jnp.logical_not(takes))
        def _():
            result[...] = jnp.zeros_like(result)

        if pairs > 1:
            first = 0 if ph == 0 else pairs - 1

            @pl.when(upstream(ph, first))
            def _():
                from_pair(ph, first).wait_recv()
                fs[ph] = qbuf[ph, first]
                for source in range(pairs):
                    if source != first:
                        @pl.when(upstream(ph, source))
                        def _():
                            from_pair(ph, source).wait_recv()
                            fs[ph] = fs[ph] + qbuf[ph, source]
                forward(ph).start()
                result[own_rows, :] = result[own_rows, :] + fs[ph]
                forward(ph).wait_recv()
                result[other_rows, :] = result[other_rows, :] + fbuf[ph]

    def exchange_sent(ph):
        to_partner(ph, 0).wait_send()
        to_partner(ph, 1).wait_send()
        if pairs > 1:
            for target in range(pairs):
                @pl.when(downstream(ph, target))
                def _():
                    to_pair(ph, target).wait_send()

            @pl.when(upstream(ph, 0 if ph == 0 else pairs - 1))
            def _():
                forward(ph).wait_send()

    exchange_begin(0)

    def weigh(i, carry):
        rows = pl.ds(pl.multiple_of(i * ROWS, ROWS), ROWS)
        for j in range(lane_blocks):
            lanes = pl.ds(j * LANES, LANES)
            rate = -absorb[:, lanes]
            prior = w[0, rows, lanes]
            for b in range(1, cells):
                c = w[b, rows, lanes]
                w[b, rows, lanes] = c * jnp.exp(rate * prior)
                prior = prior + c
        return carry

    lax.fori_loop(0, tiles, weigh, 0)

    exchange_end(0, before)
    light_out[...] = entry[...] * jnp.exp(-absorb[...] * before[...])

    def emit(g, carry):
        for j in range(lane_blocks):
            lanes = pl.ds(j * LANES, LANES)
            sums = []
            for r in range(ROWS):
                acc = [None, None]
                for t in range(tiles):
                    rows = pl.ds(t * ROWS, ROWS)
                    term = light_out[rows, lanes] * w[g * ROWS + r, rows, lanes]
                    acc[t % 2] = term if acc[t % 2] is None else acc[t % 2] + term
                sums.append(jnp.sum(acc[0] + acc[1], axis=0, keepdims=True))
            img[g * lane_blocks + j] = jnp.concatenate(sums, axis=0)
        return carry

    lax.fori_loop(0, cells // ROWS, emit, 0)

    def guarded(index, body):
        if owners == nd:
            body()
        else:
            pl.when(index < owners)(body)

    def scatter(target, k):
        return pltpu.make_async_remote_copy(
            src_ref=img.at[pl.ds(target * per, per)],
            dst_ref=rs.at[di],
            send_sem=rs_send.at[k],
            recv_sem=rs_recv.at[di],
            device_id={"depth": target},
            device_id_type=MESH,
        )

    def scattered(source, k):
        return pltpu.make_async_remote_copy(
            src_ref=img.at[pl.ds(0, per)],
            dst_ref=rs.at[source],
            send_sem=rs_send.at[k],
            recv_sem=rs_recv.at[source],
            device_id={"depth": source},
            device_id_type=MESH,
        )

    def gather(target, k):
        mine = pl.ds(di * per, per)
        return pltpu.make_async_remote_copy(
            src_ref=ag.at[mine],
            dst_ref=ag.at[mine],
            send_sem=ag_send.at[k],
            recv_sem=ag_recv.at[di],
            device_id={"depth": target},
            device_id_type=MESH,
        )

    def gathered(source, k):
        theirs = pl.ds(source * per, per)
        return pltpu.make_async_remote_copy(
            src_ref=ag.at[theirs],
            dst_ref=ag.at[theirs],
            send_sem=ag_send.at[k],
            recv_sem=ag_recv.at[source],
            device_id={"depth": source},
            device_id_type=MESH,
        )

    for k in range(1, nd):
        target = lax.rem(di + k, nd)
        guarded(target, lambda target=target, k=k: scatter(target, k).start())

    def reduce_own():
        total = img[pl.ds(di * per, per)]
        for k in range(1, nd):
            source = lax.rem(di + k, nd)
            scattered(source, k).wait_recv()
            total = total + rs[source]
        ag[pl.ds(di * per, per)] = total * (1.0 / (depth * nd))
        for k in range(1, nd):
            gather(lax.rem(di + k, nd), k).start()

    guarded(di, reduce_own)

    for k in range(1, nd):
        source = lax.rem(di + k, nd)
        guarded(source, lambda source=source, k=k: gathered(source, k).wait_recv())

    image = jnp.concatenate(
        [
            jnp.concatenate([ag[g * lane_blocks + j] for j in range(lane_blocks)], axis=1)
            for g in range(cells // ROWS)
        ],
        axis=0,
    )
    taps = [taps_ref[k] for k in range(5)]
    residual = blur(image, taps, 1) - measured[...]
    res_out[...] = residual
    back_out[...] = blur(residual, taps, -1)

    def weighted(i, carry):
        rows = pl.ds(pl.multiple_of(i * ROWS, ROWS), ROWS)
        parts = [back_out[b:b + 1, :] * w[b, rows, :] for b in range(4)]
        for b in range(4, cells):
            parts[b % 4] = parts[b % 4] + back_out[b:b + 1, :] * w[b, rows, :]
        tot[1, rows, :] = light_out[rows, :] * ((parts[0] + parts[1]) + (parts[2] + parts[3]))
        return carry

    lax.fori_loop(0, tiles, weighted, 0)
    exchange_begin(1)
    exchange_end(1, after_out)

    exchange_sent(0)
    exchange_sent(1)
    for k in range(1, nd):
        target = lax.rem(di + k, nd)
        guarded(target, lambda target=target, k=k: scatter(target, k).wait_send())

    def sent():
        for k in range(1, nd):
            gather(lax.rem(di + k, nd), k).wait_send()

    guarded(di, sent)


def exchange(nb, nd, concentration, entry, absorb, taps, measured):
    cells, depth, height = concentration.shape
    half, pairs = depth // 2, nb // 2
    pieces = (cells // ROWS) * (height // LANES)
    per = pieces // min(nd, pieces)
    f32 = jnp.float32
    dma = pltpu.SemaphoreType.DMA
    vmem = pl.BlockSpec(memory_space=pltpu.VMEM)
    return pl.pallas_call(
        functools.partial(exchange_kernel, nb, nd),
        out_shape=[
            jax.ShapeDtypeStruct((depth, height), f32),
            jax.ShapeDtypeStruct((cells, height), f32),
            jax.ShapeDtypeStruct((depth, height), f32),
            jax.ShapeDtypeStruct((cells, height), f32),
        ],
        in_specs=[
            pl.BlockSpec(memory_space=pl.ANY), vmem, vmem,
            pl.BlockSpec(memory_space=pltpu.SMEM), vmem,
        ],
        out_specs=[vmem] * 4,
        scratch_shapes=[
            pltpu.VMEM((cells, depth, height), f32),
            pltpu.VMEM((2, depth, height), f32),
            pltpu.VMEM((2, 2, half, height), f32),
            pltpu.VMEM((2, half, height), f32),
            pltpu.VMEM((2, pairs, half, height), f32),
            pltpu.VMEM((2, half, height), f32),
            pltpu.VMEM((2, half, height), f32),
            pltpu.VMEM((depth, height), f32),
            pltpu.VMEM((pieces, ROWS, LANES), f32),
            pltpu.VMEM((nd, per, ROWS, LANES), f32),
            pltpu.VMEM((pieces, ROWS, LANES), f32),
            dma((CHUNKS,)), dma((2, 2)), dma((2, 2)),
            dma((2, pairs)), dma((2, pairs)), dma((2,)), dma((2,)),
            dma((nd,)), dma((nd,)), dma((nd,)), dma((nd,)),
        ],
        compiler_params=pltpu.CompilerParams(
            collective_id=0, has_side_effects=True, vmem_limit_bytes=24 * 2**20
        ),
        name="exchange",
    )(concentration, entry, absorb, taps, measured)


def descent_kernel(nd, c_ref, light_ref, after_ref, back_ref, absorb_ref, res_ref, out_ref, res_out):
    cells, depth, height = c_ref.shape
    width = height // nd

    @pl.when(pl.program_id(0) == 0)
    def _():
        di = lax.axis_index("depth")
        for k in range(nd):
            @pl.when(di == k)
            def _():
                res_out[...] = res_ref[:, k * width:(k + 1) * width]

    def tile(i, carry):
        rows = pl.ds(pl.multiple_of(i * ROWS, ROWS), ROWS)
        for j in range(height // LANES):
            lanes = pl.ds(j * LANES, LANES)
            rate = absorb_ref[:, lanes]
            light = light_ref[rows, lanes]
            prior = None
            q = []
            for b in range(cells):
                trans = light if prior is None else light * jnp.exp(-rate * prior)
                q.append(back_ref[b:b + 1, lanes] * trans)
                c = c_ref[b, rows, lanes]
                prior = c if prior is None else prior + c
            later = after_ref[rows, lanes]
            for b in reversed(range(cells)):
                out_ref[b, rows, lanes] = rate * later - q[b]
                later = later + q[b] * c_ref[b, rows, lanes]
        return carry

    lax.fori_loop(0, depth // ROWS, tile, 0)


def write_descent(nd, concentration, light, after, back, absorb, residual):
    cells, depth, height = concentration.shape
    block = 2 * ROWS
    big = pl.BlockSpec((cells, block, height), lambda i: (0, i, 0))
    flat = pl.BlockSpec((block, height), lambda i: (i, 0))
    whole = lambda shape: pl.BlockSpec(shape, lambda i: (0, 0))
    return pl.pallas_call(
        functools.partial(descent_kernel, nd),
        grid=(depth // block,),
        out_shape=[
            jax.ShapeDtypeStruct(concentration.shape, jnp.float32),
            jax.ShapeDtypeStruct((cells, height // nd), jnp.float32),
        ],
        in_specs=[big, flat, flat, whole(back.shape), whole(absorb.shape), whole(residual.shape)],
        out_specs=[big, whole((cells, height // nd))],
        compiler_params=pltpu.CompilerParams(vmem_limit_bytes=24 * 2**20),
        name="descent",
    )(concentration, light, after, back, absorb, residual)


def solution(mesh):
    nb, nd = mesh.shape["beam"], mesh.shape["depth"]

    def local(concentration, entry_intensity, absorb, blur_taps, measured):
        absorb = absorb.reshape(1, -1)
        light, back, after, residual = exchange(
            nb, nd, concentration, entry_intensity, absorb, blur_taps, measured
        )
        return tuple(write_descent(nd, concentration, light, after, back, absorb, residual))

    return jax.shard_map(
        local,
        mesh=mesh,
        in_specs=(P("beam", "depth", None), P("depth", None), P(), P(), P("beam", None)),
        out_specs=(P("beam", "depth", None), P("beam", "depth")),
        check_vma=False,
    )
```

```python
import functools

import jax
import jax.numpy as jnp
from jax import lax
from jax.experimental import pallas as pl
from jax.experimental.pallas import tpu as pltpu
from jax.sharding import PartitionSpec as P

MESH = pl.DeviceIdType.MESH
ROWS, LANES = 8, 128
SUBS = 2
WRITES = 8


def blur(x, taps, sign):
    width = x.shape[1]
    lane = lax.broadcasted_iota(jnp.int32, x.shape, 1)
    total = jnp.zeros_like(x)
    for k in range(5):
        step = sign * (k - 2)
        moved = x if step == 0 else pltpu.roll(x, (-step) % width, 1)
        inside = (lane + step >= 0) & (lane + step < width)
        total = total + taps[k] * jnp.where(inside, moved, 0.0)
    return total


def exchange_kernel(
    nb, nd, c_hbm, entry_hbm, absorb_hbm, taps_hbm, measured_hbm,
    trans, later_out, res_out,
    w, entry, absorb, taps_ref, measured, light, wide, tot, pbuf, ps, qbuf, fs, fbuf, before,
    img, rs, ag,
    load_sem, small_sem, a_send, a_recv, b_send, b_recv, f_send, f_recv,
    rs_send, rs_recv, ag_send, ag_recv,
):
    cells, depth, height = w.shape
    half = depth // 2
    sub = half // SUBS
    pairs = nb // 2
    bi = lax.axis_index("beam")
    di = lax.axis_index("depth")
    core = lax.rem(bi, 2)
    pair = bi // 2
    partner = bi + 1 - 2 * core
    tiles = depth // ROWS
    lane_blocks = height // LANES
    pieces = (cells // ROWS) * lane_blocks
    owners = min(nd, pieces)
    per = pieces // owners

    own_start = pl.multiple_of(core * half, ROWS)
    other_start = pl.multiple_of((1 - core) * half, ROWS)
    own_rows = pl.ds(own_start, half)
    other_rows = pl.ds(other_start, half)

    def at(start, s):
        return pl.ds(pl.multiple_of(start + s * sub, ROWS), sub)

    loads = []
    for start in (other_start, own_start):
        for s in range(SUBS):
            part = at(start, s)
            copy = pltpu.make_async_copy(
                c_hbm.at[:, part, :], w.at[:, part, :], load_sem.at[len(loads)]
            )
            copy.start()
            loads.append(copy)
    small = []
    for source, place in (
        (absorb_hbm, absorb), (entry_hbm, entry), (taps_hbm, taps_ref), (measured_hbm, measured)
    ):
        copy = pltpu.make_async_copy(source, place, small_sem.at[len(small)])
        copy.start()
        small.append(copy)

    barrier = pltpu.get_barrier_semaphore()
    for k in range(1, nb):
        pl.semaphore_signal(
            barrier, inc=1, device_id={"beam": lax.rem(bi + k, nb)}, device_id_type=MESH
        )
    for k in range(1, nd):
        pl.semaphore_signal(
            barrier, inc=1, device_id={"depth": lax.rem(di + k, nd)}, device_id_type=MESH
        )

    def sum_cells(start, s):
        def tile(i, carry):
            rows = pl.ds(pl.multiple_of(start + s * sub + i * ROWS, ROWS), ROWS)
            parts = [w[b, rows, :] for b in range(4)]
            for b in range(4, cells):
                parts[b % 4] = parts[b % 4] + w[b, rows, :]
            tot[0, rows, :] = (parts[0] + parts[1]) + (parts[2] + parts[3])
            return carry

        lax.fori_loop(0, sub // ROWS, tile, 0)

    def sum_weighted(start, s):
        rows = [
            pl.ds(pl.multiple_of(start + s * sub + i * ROWS, ROWS), ROWS)
            for i in range(sub // ROWS)
        ]
        for j in range(lane_blocks):
            lanes = pl.ds(j * LANES, LANES)
            acc = None
            for b in range(cells):
                factor = wide[b, :, lanes]
                terms = [factor * w[b, r, lanes] for r in rows]
                acc = terms if acc is None else [x + y for x, y in zip(acc, terms)]
            for r, x in zip(rows, acc):
                tot[1, r, lanes] = light[r, lanes] * x

    def to_partner(ph, slot):
        return pltpu.make_async_remote_copy(
            src_ref=tot.at[ph, other_rows if slot == 0 else own_rows, :],
            dst_ref=pbuf.at[ph, slot],
            send_sem=a_send.at[ph, slot],
            recv_sem=a_recv.at[ph, slot],
            device_id={"beam": partner},
            device_id_type=MESH,
        )

    def to_pair(ph, target, s):
        return pltpu.make_async_remote_copy(
            src_ref=ps.at[ph, s],
            dst_ref=qbuf.at[ph, pair, s],
            send_sem=b_send.at[ph, target, s],
            recv_sem=b_recv.at[ph, pair, s],
            device_id={"beam": 2 * target + core},
            device_id_type=MESH,
        )

    def from_pair(ph, source, s):
        return pltpu.make_async_remote_copy(
            src_ref=ps.at[ph, s],
            dst_ref=qbuf.at[ph, source, s],
            send_sem=b_send.at[ph, source, s],
            recv_sem=b_recv.at[ph, source, s],
            device_id={"beam": 2 * source + core},
            device_id_type=MESH,
        )

    def forward(ph, s):
        return pltpu.make_async_remote_copy(
            src_ref=fs.at[ph, s],
            dst_ref=fbuf.at[ph, s],
            send_sem=f_send.at[ph, s],
            recv_sem=f_recv.at[ph, s],
            device_id={"beam": partner},
            device_id_type=MESH,
        )

    def downstream(ph, other):
        return other > pair if ph == 0 else other < pair

    def upstream(ph, other):
        return other < pair if ph == 0 else other > pair

    def exchange_begin(ph, sums):
        for s in range(SUBS):
            sums(other_start, s)
        if ph == 0:
            pl.semaphore_wait(barrier, nb - 1 + nd - 1)
        to_partner(ph, 0).start()
        for s in range(SUBS):
            sums(own_start, s)
            if s == 0:
                to_partner(ph, 0).wait_recv()
            if pairs > 1:
                ps[ph, s] = tot[ph, at(own_start, s), :] + pbuf[ph, 0, s * sub:(s + 1) * sub, :]
                for target in range(pairs):
                    @pl.when(downstream(ph, target))
                    def _():
                        to_pair(ph, target, s).start()
        to_partner(ph, 1).start()

    def exchange_end(ph, result):
        first = 0 if ph == 0 else pairs - 1
        if pairs > 1:
            @pl.when(upstream(ph, first))
            def _():
                for s in range(SUBS):
                    from_pair(ph, first, s).wait_recv()
                    fs[ph, s] = qbuf[ph, first, s]
                    for source in range(pairs):
                        if source != first:
                            @pl.when(upstream(ph, source))
                            def _():
                                from_pair(ph, source, s).wait_recv()
                                fs[ph, s] = fs[ph, s] + qbuf[ph, source, s]
                    forward(ph, s).start()

        to_partner(ph, 1).wait_recv()
        takes = core == (1 if ph == 0 else 0)

        @pl.when(takes)
        def _():
            result[own_rows, :] = pbuf[ph, 0]
            result[other_rows, :] = pbuf[ph, 1]

        @pl.when(jnp.logical_not(takes))
        def _():
            result[...] = jnp.zeros_like(result)

        if pairs > 1:
            @pl.when(upstream(ph, first))
            def _():
                for s in range(SUBS):
                    mine, theirs = at(own_start, s), at(other_start, s)
                    result[mine, :] = result[mine, :] + fs[ph, s]
                    forward(ph, s).wait_recv()
                    result[theirs, :] = result[theirs, :] + fbuf[ph, s]

    def exchange_sent(ph):
        to_partner(ph, 0).wait_send()
        to_partner(ph, 1).wait_send()
        if pairs > 1:
            for s in range(SUBS):
                for target in range(pairs):
                    @pl.when(downstream(ph, target))
                    def _():
                        to_pair(ph, target, s).wait_send()

                @pl.when(upstream(ph, 0 if ph == 0 else pairs - 1))
                def _():
                    forward(ph, s).wait_send()

    def sum_loaded(start, s):
        loads[s if start is other_start else SUBS + s].wait()
        sum_cells(start, s)

    exchange_begin(0, sum_loaded)
    for copy in small:
        copy.wait()

    def weigh(i, carry):
        rows = pl.ds(pl.multiple_of(i * ROWS, ROWS), ROWS)
        for j in range(lane_blocks):
            lanes = pl.ds(j * LANES, LANES)
            rate = -absorb[:, lanes]
            prior = w[0, rows, lanes]
            for b in range(1, cells):
                c = w[b, rows, lanes]
                passed = jnp.exp(rate * prior)
                trans[b, rows, lanes] = passed
                w[b, rows, lanes] = c * passed
                prior = prior + c
        return carry

    lax.fori_loop(0, tiles, weigh, 0)

    exchange_end(0, before)
    light[...] = entry[...] * jnp.exp(-absorb[...] * before[...])

    def emit(g, carry):
        for j in range(lane_blocks):
            lanes = pl.ds(j * LANES, LANES)
            sums = []
            for r in range(ROWS):
                acc = [None, None]
                for t in range(tiles):
                    rows = pl.ds(t * ROWS, ROWS)
                    term = light[rows, lanes] * w[g * ROWS + r, rows, lanes]
                    acc[t % 2] = term if acc[t % 2] is None else acc[t % 2] + term
                sums.append(jnp.sum(acc[0] + acc[1], axis=0, keepdims=True))
            img[g * lane_blocks + j] = jnp.concatenate(sums, axis=0)
        return carry

    lax.fori_loop(0, cells // ROWS, emit, 0)

    def guarded(index, body):
        if owners == nd:
            body()
        else:
            pl.when(index < owners)(body)

    def scatter(target, k):
        return pltpu.make_async_remote_copy(
            src_ref=img.at[pl.ds(target * per, per)],
            dst_ref=rs.at[di],
            send_sem=rs_send.at[k],
            recv_sem=rs_recv.at[di],
            device_id={"depth": target},
            device_id_type=MESH,
        )

    def scattered(source, k):
        return pltpu.make_async_remote_copy(
            src_ref=img.at[pl.ds(0, per)],
            dst_ref=rs.at[source],
            send_sem=rs_send.at[k],
            recv_sem=rs_recv.at[source],
            device_id={"depth": source},
            device_id_type=MESH,
        )

    def gather(target, k):
        mine = pl.ds(di * per, per)
        return pltpu.make_async_remote_copy(
            src_ref=ag.at[mine],
            dst_ref=ag.at[mine],
            send_sem=ag_send.at[k],
            recv_sem=ag_recv.at[di],
            device_id={"depth": target},
            device_id_type=MESH,
        )

    def gathered(source, k):
        theirs = pl.ds(source * per, per)
        return pltpu.make_async_remote_copy(
            src_ref=ag.at[theirs],
            dst_ref=ag.at[theirs],
            send_sem=ag_send.at[k],
            recv_sem=ag_recv.at[source],
            device_id={"depth": source},
            device_id_type=MESH,
        )

    for k in range(1, nd):
        target = lax.rem(di + k, nd)
        guarded(target, lambda target=target, k=k: scatter(target, k).start())

    def reduce_own():
        total = img[pl.ds(di * per, per)]
        for k in range(1, nd):
            source = lax.rem(di + k, nd)
            scattered(source, k).wait_recv()
            total = total + rs[source]
        ag[pl.ds(di * per, per)] = total * (1.0 / (depth * nd))
        for k in range(1, nd):
            gather(lax.rem(di + k, nd), k).start()

    guarded(di, reduce_own)

    for k in range(1, nd):
        source = lax.rem(di + k, nd)
        guarded(source, lambda source=source, k=k: gathered(source, k).wait_recv())

    image = jnp.concatenate(
        [
            jnp.concatenate([ag[g * lane_blocks + j] for j in range(lane_blocks)], axis=1)
            for g in range(cells // ROWS)
        ],
        axis=0,
    )
    taps = [taps_ref[k] for k in range(5)]
    residual = blur(image, taps, 1) - measured[...]
    res_out[...] = residual
    back = blur(residual, taps, -1)
    for b in range(cells):
        wide[b] = jnp.broadcast_to(back[b:b + 1, :], (ROWS, height))

    exchange_begin(1, sum_weighted)

    def adjoint(i, carry):
        rows = pl.ds(pl.multiple_of(i * ROWS, ROWS), ROWS)
        for j in range(lane_blocks):
            lanes = pl.ds(j * LANES, LANES)
            rate, lamp = absorb[:, lanes], light[rows, lanes]
            later = None
            for b in reversed(range(cells)):
                scale = lamp * wide[b, :, lanes]
                q = scale if b == 0 else scale * trans[b, rows, lanes]
                trans[b, rows, lanes] = -q if later is None else rate * later - q
                if b > 0:
                    term = scale * w[b, rows, lanes]
                    later = term if later is None else later + term
        return carry

    lax.fori_loop(0, tiles, adjoint, 0)
    exchange_end(1, before)
    later_out[...] = absorb[...] * before[...]

    exchange_sent(0)
    exchange_sent(1)
    for k in range(1, nd):
        target = lax.rem(di + k, nd)
        guarded(target, lambda target=target, k=k: scatter(target, k).wait_send())

    def sent():
        for k in range(1, nd):
            gather(lax.rem(di + k, nd), k).wait_send()

    guarded(di, sent)


def in_hbm(x):
    return pltpu.with_memory_space_constraint(x, pltpu.HBM)


def exchange(nb, nd, concentration, entry, absorb, taps, measured):
    cells, depth, height = concentration.shape
    half, pairs = depth // 2, nb // 2
    sub = half // SUBS
    pieces = (cells // ROWS) * (height // LANES)
    per = pieces // min(nd, pieces)
    f32 = jnp.float32
    dma = pltpu.SemaphoreType.DMA
    vmem = pl.BlockSpec(memory_space=pltpu.VMEM)
    return pl.pallas_call(
        functools.partial(exchange_kernel, nb, nd),
        out_shape=[
            jax.ShapeDtypeStruct((cells, depth, height), f32),
            jax.ShapeDtypeStruct((depth, height), f32),
            jax.ShapeDtypeStruct((cells, height), f32),
        ],
        in_specs=[pl.BlockSpec(memory_space=pltpu.HBM)] * 5,
        out_specs=[vmem] * 3,
        scratch_shapes=[
            pltpu.VMEM((cells, depth, height), f32),
            pltpu.VMEM((depth, height), f32),
            pltpu.VMEM(absorb.shape, f32),
            pltpu.SMEM(taps.shape, f32),
            pltpu.VMEM((cells, height), f32),
            pltpu.VMEM((depth, height), f32),
            pltpu.VMEM((cells, ROWS, height), f32),
            pltpu.VMEM((2, depth, height), f32),
            pltpu.VMEM((2, 2, half, height), f32),
            pltpu.VMEM((2, SUBS, sub, height), f32),
            pltpu.VMEM((2, pairs, SUBS, sub, height), f32),
            pltpu.VMEM((2, SUBS, sub, height), f32),
            pltpu.VMEM((2, SUBS, sub, height), f32),
            pltpu.VMEM((depth, height), f32),
            pltpu.VMEM((pieces, ROWS, LANES), f32),
            pltpu.VMEM((nd, per, ROWS, LANES), f32),
            pltpu.VMEM((pieces, ROWS, LANES), f32),
            dma((2 * SUBS,)), dma((4,)), dma((2, 2)), dma((2, 2)),
            dma((2, pairs, SUBS)), dma((2, pairs, SUBS)), dma((2, SUBS)), dma((2, SUBS)),
            dma((nd,)), dma((nd,)), dma((nd,)), dma((nd,)),
        ],
        compiler_params=pltpu.CompilerParams(
            collective_id=0, has_side_effects=True, vmem_limit_bytes=24 * 2**20
        ),
        name="exchange",
    )(*(in_hbm(x) for x in (concentration, entry, absorb, taps, measured)))


def descent_kernel(nd, part_ref, later_ref, res_ref, out_hbm, res_hbm, stage, res_stage, sems, res_sem):
    cells, depth, height = part_ref.shape
    width = height // nd
    di = lax.axis_index("depth")
    group = cells // WRITES

    for n in range(WRITES):
        def tile(i, carry):
            rows = pl.ds(pl.multiple_of(i * ROWS, ROWS), ROWS)
            later = later_ref[rows, :]
            for b in range(n * group, (n + 1) * group):
                stage[b, rows, :] = part_ref[b, rows, :] + later
            return carry

        lax.fori_loop(0, depth // ROWS, tile, 0)
        part = pl.ds(n * group, group)
        pltpu.make_async_copy(stage.at[part], out_hbm.at[part], sems.at[n]).start()

    for k in range(nd):
        @pl.when(di == k)
        def _():
            res_stage[...] = res_ref[:, k * width:(k + 1) * width]
    residual = pltpu.make_async_copy(res_stage, res_hbm, res_sem.at[0])
    residual.start()
    for n in range(WRITES):
        part = pl.ds(n * group, group)
        pltpu.make_async_copy(stage.at[part], out_hbm.at[part], sems.at[n]).wait()
    residual.wait()


def write_descent(nd, part, later, residual):
    cells, depth, height = part.shape
    f32 = jnp.float32
    shapes = (part.shape, (cells, height // nd))
    return pl.pallas_call(
        functools.partial(descent_kernel, nd),
        out_shape=[jax.ShapeDtypeStruct(shape, f32) for shape in shapes],
        in_specs=[pl.BlockSpec(memory_space=pltpu.VMEM)] * 3,
        out_specs=[pl.BlockSpec(memory_space=pltpu.HBM)] * 2,
        scratch_shapes=[
            pltpu.VMEM(shapes[0], f32),
            pltpu.VMEM(shapes[1], f32),
            pltpu.SemaphoreType.DMA((WRITES,)),
            pltpu.SemaphoreType.DMA((1,)),
        ],
        compiler_params=pltpu.CompilerParams(vmem_limit_bytes=24 * 2**20),
        name="descent",
    )(part, later, residual)


def solution(mesh):
    nb, nd = mesh.shape["beam"], mesh.shape["depth"]

    def local(concentration, entry_intensity, absorb, blur_taps, measured):
        part, later, residual = exchange(
            nb, nd, concentration, entry_intensity, absorb.reshape(1, -1), blur_taps, measured
        )
        return tuple(write_descent(nd, part, later, residual))

    return jax.shard_map(
        local,
        mesh=mesh,
        in_specs=(P("beam", "depth", None), P("depth", None), P(), P(), P("beam", None)),
        out_specs=(P("beam", "depth", None), P("beam", "depth")),
        check_vma=False,
    )
```

```python
import functools

import jax
import jax.numpy as jnp
from jax import lax
from jax.experimental import pallas as pl
from jax.experimental.pallas import tpu as pltpu
from jax.sharding import PartitionSpec as P

MESH = pl.DeviceIdType.MESH
ROWS, LANES = 8, 128
SUBS = 4
DIRECT = 2
WRITES = 8


def blur(x, taps, sign):
    width = x.shape[1]
    lane = lax.broadcasted_iota(jnp.int32, x.shape, 1)
    total = jnp.zeros_like(x)
    for k in range(5):
        step = sign * (k - 2)
        moved = x if step == 0 else pltpu.roll(x, (-step) % width, 1)
        inside = (lane + step >= 0) & (lane + step < width)
        total = total + taps[k] * jnp.where(inside, moved, 0.0)
    return total


def exchange_kernel(
    nb, nd, c_hbm, entry_hbm, absorb_hbm, taps_hbm, measured_hbm,
    trans, later_out, res_out,
    w, entry, absorb, taps_ref, measured, light, wide, tot, pbuf, ps, qbuf, dbuf, fs, fbuf, before,
    img, rs, ag,
    load_sem, small_sem, a_send, a_recv, b_send, b_recv, d_send, d_recv, f_send, f_recv,
    rs_send, rs_recv, ag_send, ag_recv,
):
    cells, depth, height = w.shape
    half = depth // 2
    sub = half // SUBS
    relayed = SUBS - DIRECT
    pairs = nb // 2
    bi = lax.axis_index("beam")
    di = lax.axis_index("depth")
    core = lax.rem(bi, 2)
    pair = bi // 2
    partner = bi + 1 - 2 * core
    tiles = depth // ROWS
    lane_blocks = height // LANES
    pieces = (cells // ROWS) * lane_blocks
    owners = min(nd, pieces)
    per = pieces // owners

    own_start = pl.multiple_of(core * half, ROWS)
    other_start = pl.multiple_of((1 - core) * half, ROWS)
    own_rows = pl.ds(own_start, half)
    other_rows = pl.ds(other_start, half)

    def at(start, s):
        return pl.ds(pl.multiple_of(start + s * sub, ROWS), sub)

    loads = []
    for start in (other_start, own_start):
        for s in range(SUBS):
            part = at(start, s)
            copy = pltpu.make_async_copy(
                c_hbm.at[:, part, :], w.at[:, part, :], load_sem.at[len(loads)]
            )
            copy.start()
            loads.append(copy)
    small = []
    for source, place in (
        (absorb_hbm, absorb), (entry_hbm, entry), (taps_hbm, taps_ref), (measured_hbm, measured)
    ):
        copy = pltpu.make_async_copy(source, place, small_sem.at[len(small)])
        copy.start()
        small.append(copy)

    barrier = pltpu.get_barrier_semaphore()
    for k in range(1, nb):
        pl.semaphore_signal(
            barrier, inc=1, device_id={"beam": lax.rem(bi + k, nb)}, device_id_type=MESH
        )
    for k in range(1, nd):
        pl.semaphore_signal(
            barrier, inc=1, device_id={"depth": lax.rem(di + k, nd)}, device_id_type=MESH
        )

    def sum_cells(start, s):
        def tile(i, carry):
            rows = pl.ds(pl.multiple_of(start + s * sub + i * ROWS, ROWS), ROWS)
            parts = [w[b, rows, :] for b in range(4)]
            for b in range(4, cells):
                parts[b % 4] = parts[b % 4] + w[b, rows, :]
            tot[0, rows, :] = (parts[0] + parts[1]) + (parts[2] + parts[3])
            return carry

        lax.fori_loop(0, sub // ROWS, tile, 0)

    def sum_weighted(start, s):
        rows = [
            pl.ds(pl.multiple_of(start + s * sub + i * ROWS, ROWS), ROWS)
            for i in range(sub // ROWS)
        ]
        for j in range(lane_blocks):
            lanes = pl.ds(j * LANES, LANES)
            acc = None
            for b in range(cells):
                factor = wide[b, :, lanes]
                terms = [factor * w[b, r, lanes] for r in rows]
                acc = terms if acc is None else [x + y for x, y in zip(acc, terms)]
            for r, x in zip(rows, acc):
                tot[1, r, lanes] = light[r, lanes] * x

    def to_partner(ph, slot):
        return pltpu.make_async_remote_copy(
            src_ref=tot.at[ph, other_rows if slot == 0 else own_rows, :],
            dst_ref=pbuf.at[ph, slot],
            send_sem=a_send.at[ph, slot],
            recv_sem=a_recv.at[ph, slot],
            device_id={"beam": partner},
            device_id_type=MESH,
        )

    def to_pair(ph, target, s):
        return pltpu.make_async_remote_copy(
            src_ref=ps.at[ph, s],
            dst_ref=qbuf.at[ph, pair, s],
            send_sem=b_send.at[ph, target, s],
            recv_sem=b_recv.at[ph, pair, s],
            device_id={"beam": 2 * target + core},
            device_id_type=MESH,
        )

    def from_pair(ph, source, s):
        return pltpu.make_async_remote_copy(
            src_ref=ps.at[ph, s],
            dst_ref=qbuf.at[ph, source, s],
            send_sem=b_send.at[ph, source, s],
            recv_sem=b_recv.at[ph, source, s],
            device_id={"beam": 2 * source + core},
            device_id_type=MESH,
        )

    def to_cross(ph, target, s):
        return pltpu.make_async_remote_copy(
            src_ref=ps.at[ph, s],
            dst_ref=dbuf.at[ph, pair, s - relayed],
            send_sem=d_send.at[ph, target, s - relayed],
            recv_sem=d_recv.at[ph, pair, s - relayed],
            device_id={"beam": 2 * target + 1 - core},
            device_id_type=MESH,
        )

    def from_cross(ph, source, s):
        return pltpu.make_async_remote_copy(
            src_ref=ps.at[ph, s],
            dst_ref=dbuf.at[ph, source, s - relayed],
            send_sem=d_send.at[ph, source, s - relayed],
            recv_sem=d_recv.at[ph, source, s - relayed],
            device_id={"beam": 2 * source + 1 - core},
            device_id_type=MESH,
        )

    def forward(ph, s):
        return pltpu.make_async_remote_copy(
            src_ref=fs.at[ph, s],
            dst_ref=fbuf.at[ph, s],
            send_sem=f_send.at[ph, s],
            recv_sem=f_recv.at[ph, s],
            device_id={"beam": partner},
            device_id_type=MESH,
        )

    def downstream(ph, other):
        return other > pair if ph == 0 else other < pair

    def upstream(ph, other):
        return other < pair if ph == 0 else other > pair

    def exchange_begin(ph, sums):
        for s in range(SUBS):
            sums(other_start, s)
        if ph == 0:
            pl.semaphore_wait(barrier, nb - 1 + nd - 1)
        to_partner(ph, 0).start()
        for s in range(SUBS):
            sums(own_start, s)
            if s == 0:
                to_partner(ph, 0).wait_recv()
            if pairs > 1:
                ps[ph, s] = tot[ph, at(own_start, s), :] + pbuf[ph, 0, s * sub:(s + 1) * sub, :]
                for target in range(pairs):
                    @pl.when(downstream(ph, target))
                    def _():
                        to_pair(ph, target, s).start()
                        if s >= relayed:
                            to_cross(ph, target, s).start()
        to_partner(ph, 1).start()

    def collect(ph, s):
        first = 0 if ph == 0 else pairs - 1
        from_pair(ph, first, s).wait_recv()
        fs[ph, s] = qbuf[ph, first, s]
        for source in range(pairs):
            if source != first:
                @pl.when(upstream(ph, source))
                def _():
                    from_pair(ph, source, s).wait_recv()
                    fs[ph, s] = fs[ph, s] + qbuf[ph, source, s]

    def when_upstream(ph, body):
        if pairs > 1:
            pl.when(upstream(ph, 0 if ph == 0 else pairs - 1))(body)

    def relay(ph):
        def body():
            for s in range(relayed):
                collect(ph, s)
                forward(ph, s).start()

        when_upstream(ph, body)

    def from_core(ph, slot, result):
        takes = core == (1 if ph == 0 else 0)
        rows = own_rows if slot == 0 else other_rows

        @pl.when(takes)
        def _():
            result[rows, :] = pbuf[ph, slot]

        @pl.when(jnp.logical_not(takes))
        def _():
            result[rows, :] = jnp.zeros((half, height), jnp.float32)

    def finish_own(ph, result):
        from_core(ph, 0, result)

        def body():
            for s in range(SUBS):
                if s >= relayed:
                    collect(ph, s)
                rows = at(own_start, s)
                result[rows, :] = result[rows, :] + fs[ph, s]

        when_upstream(ph, body)

    def finish_other(ph, result):
        to_partner(ph, 1).wait_recv()
        from_core(ph, 1, result)

        def body():
            for s in range(SUBS):
                rows = at(other_start, s)
                if s < relayed:
                    forward(ph, s).wait_recv()
                    result[rows, :] = result[rows, :] + fbuf[ph, s]
                else:
                    for source in range(pairs):
                        @pl.when(upstream(ph, source))
                        def _():
                            from_cross(ph, source, s).wait_recv()
                            result[rows, :] = result[rows, :] + dbuf[ph, source, s - relayed]

        when_upstream(ph, body)

    def exchange_sent(ph):
        to_partner(ph, 0).wait_send()
        to_partner(ph, 1).wait_send()
        if pairs > 1:
            for s in range(SUBS):
                for target in range(pairs):
                    @pl.when(downstream(ph, target))
                    def _():
                        to_pair(ph, target, s).wait_send()
                        if s >= relayed:
                            to_cross(ph, target, s).wait_send()

            @pl.when(upstream(ph, 0 if ph == 0 else pairs - 1))
            def _():
                for s in range(relayed):
                    forward(ph, s).wait_send()

    def sum_loaded(start, s):
        loads[s if start is other_start else SUBS + s].wait()
        sum_cells(start, s)

    exchange_begin(0, sum_loaded)
    for copy in small:
        copy.wait()

    def weigh(start, first, last):
        def tile(i, carry):
            rows = pl.ds(pl.multiple_of(start + i * ROWS, ROWS), ROWS)
            for j in range(lane_blocks):
                lanes = pl.ds(j * LANES, LANES)
                rate = -absorb[:, lanes]
                prior = w[0, rows, lanes]
                for b in range(1, cells):
                    c = w[b, rows, lanes]
                    passed = jnp.exp(rate * prior)
                    trans[b, rows, lanes] = passed
                    w[b, rows, lanes] = c * passed
                    prior = prior + c
            return carry

        lax.fori_loop(first, last, tile, 0)

    def enter(rows):
        light[rows, :] = entry[rows, :] * jnp.exp(-absorb[...] * before[rows, :])

    def emit(start, last):
        def group(g, carry):
            for j in range(lane_blocks):
                lanes = pl.ds(j * LANES, LANES)
                tile_rows = [
                    pl.ds(pl.multiple_of(start + t * ROWS, ROWS), ROWS)
                    for t in range(half // ROWS)
                ]
                lamps = [light[rows, lanes] for rows in tile_rows]
                sums = []
                for r in range(ROWS):
                    b = g * ROWS + r
                    acc = [wide[b, :, lanes] if last else None, None]
                    for t, rows in enumerate(tile_rows):
                        term = lamps[t] * w[b, rows, lanes]
                        acc[t % 2] = term if acc[t % 2] is None else acc[t % 2] + term
                    total = acc[0] + acc[1]
                    if last:
                        sums.append(jnp.sum(total, axis=0, keepdims=True))
                    else:
                        wide[b, :, lanes] = total
                if last:
                    img[g * lane_blocks + j] = jnp.concatenate(sums, axis=0)
            return carry

        lax.fori_loop(0, cells // ROWS, group, 0)

    half_tiles = half // ROWS
    weigh(own_start, 0, half_tiles)
    weigh(other_start, 0, half_tiles // 2)
    relay(0)
    weigh(other_start, half_tiles // 2, half_tiles)
    finish_own(0, before)
    enter(own_rows)
    emit(own_start, False)
    finish_other(0, before)
    enter(other_rows)
    emit(other_start, True)

    def guarded(index, body):
        if owners == nd:
            body()
        else:
            pl.when(index < owners)(body)

    def scatter(target, k):
        return pltpu.make_async_remote_copy(
            src_ref=img.at[pl.ds(target * per, per)],
            dst_ref=rs.at[di],
            send_sem=rs_send.at[k],
            recv_sem=rs_recv.at[di],
            device_id={"depth": target},
            device_id_type=MESH,
        )

    def scattered(source, k):
        return pltpu.make_async_remote_copy(
            src_ref=img.at[pl.ds(0, per)],
            dst_ref=rs.at[source],
            send_sem=rs_send.at[k],
            recv_sem=rs_recv.at[source],
            device_id={"depth": source},
            device_id_type=MESH,
        )

    def gather(target, k):
        mine = pl.ds(di * per, per)
        return pltpu.make_async_remote_copy(
            src_ref=ag.at[mine],
            dst_ref=ag.at[mine],
            send_sem=ag_send.at[k],
            recv_sem=ag_recv.at[di],
            device_id={"depth": target},
            device_id_type=MESH,
        )

    def gathered(source, k):
        theirs = pl.ds(source * per, per)
        return pltpu.make_async_remote_copy(
            src_ref=ag.at[theirs],
            dst_ref=ag.at[theirs],
            send_sem=ag_send.at[k],
            recv_sem=ag_recv.at[source],
            device_id={"depth": source},
            device_id_type=MESH,
        )

    for k in range(1, nd):
        target = lax.rem(di + k, nd)
        guarded(target, lambda target=target, k=k: scatter(target, k).start())

    def reduce_own():
        total = img[pl.ds(di * per, per)]
        for k in range(1, nd):
            source = lax.rem(di + k, nd)
            scattered(source, k).wait_recv()
            total = total + rs[source]
        ag[pl.ds(di * per, per)] = total * (1.0 / (depth * nd))
        for k in range(1, nd):
            gather(lax.rem(di + k, nd), k).start()

    guarded(di, reduce_own)

    for k in range(1, nd):
        source = lax.rem(di + k, nd)
        guarded(source, lambda source=source, k=k: gathered(source, k).wait_recv())

    image = jnp.concatenate(
        [
            jnp.concatenate([ag[g * lane_blocks + j] for j in range(lane_blocks)], axis=1)
            for g in range(cells // ROWS)
        ],
        axis=0,
    )
    taps = [taps_ref[k] for k in range(5)]
    residual = blur(image, taps, 1) - measured[...]
    res_out[...] = residual
    back = blur(residual, taps, -1)
    for b in range(cells):
        wide[b] = jnp.broadcast_to(back[b:b + 1, :], (ROWS, height))

    exchange_begin(1, sum_weighted)

    def adjoint(i, carry):
        rows = pl.ds(pl.multiple_of(i * ROWS, ROWS), ROWS)
        for j in range(lane_blocks):
            lanes = pl.ds(j * LANES, LANES)
            rate, lamp = absorb[:, lanes], light[rows, lanes]
            later = None
            for b in reversed(range(cells)):
                scale = lamp * wide[b, :, lanes]
                q = scale if b == 0 else scale * trans[b, rows, lanes]
                trans[b, rows, lanes] = -q if later is None else rate * later - q
                if b > 0:
                    term = scale * w[b, rows, lanes]
                    later = term if later is None else later + term
        return carry

    lax.fori_loop(0, tiles, adjoint, 0)
    relay(1)
    finish_own(1, before)
    finish_other(1, before)
    later_out[...] = absorb[...] * before[...]

    exchange_sent(0)
    exchange_sent(1)
    for k in range(1, nd):
        target = lax.rem(di + k, nd)
        guarded(target, lambda target=target, k=k: scatter(target, k).wait_send())

    def sent():
        for k in range(1, nd):
            gather(lax.rem(di + k, nd), k).wait_send()

    guarded(di, sent)


def in_hbm(x):
    return pltpu.with_memory_space_constraint(x, pltpu.HBM)


def exchange(nb, nd, concentration, entry, absorb, taps, measured):
    cells, depth, height = concentration.shape
    half, pairs = depth // 2, nb // 2
    sub = half // SUBS
    pieces = (cells // ROWS) * (height // LANES)
    per = pieces // min(nd, pieces)
    f32 = jnp.float32
    dma = pltpu.SemaphoreType.DMA
    vmem = pl.BlockSpec(memory_space=pltpu.VMEM)
    return pl.pallas_call(
        functools.partial(exchange_kernel, nb, nd),
        out_shape=[
            jax.ShapeDtypeStruct((cells, depth, height), f32),
            jax.ShapeDtypeStruct((depth, height), f32),
            jax.ShapeDtypeStruct((cells, height), f32),
        ],
        in_specs=[pl.BlockSpec(memory_space=pltpu.HBM)] * 5,
        out_specs=[vmem] * 3,
        scratch_shapes=[
            pltpu.VMEM((cells, depth, height), f32),
            pltpu.VMEM((depth, height), f32),
            pltpu.VMEM(absorb.shape, f32),
            pltpu.SMEM(taps.shape, f32),
            pltpu.VMEM((cells, height), f32),
            pltpu.VMEM((depth, height), f32),
            pltpu.VMEM((cells, ROWS, height), f32),
            pltpu.VMEM((2, depth, height), f32),
            pltpu.VMEM((2, 2, half, height), f32),
            pltpu.VMEM((2, SUBS, sub, height), f32),
            pltpu.VMEM((2, pairs, SUBS, sub, height), f32),
            pltpu.VMEM((2, pairs, DIRECT, sub, height), f32),
            pltpu.VMEM((2, SUBS, sub, height), f32),
            pltpu.VMEM((2, SUBS, sub, height), f32),
            pltpu.VMEM((depth, height), f32),
            pltpu.VMEM((pieces, ROWS, LANES), f32),
            pltpu.VMEM((nd, per, ROWS, LANES), f32),
            pltpu.VMEM((pieces, ROWS, LANES), f32),
            dma((2 * SUBS,)), dma((4,)), dma((2, 2)), dma((2, 2)),
            dma((2, pairs, SUBS)), dma((2, pairs, SUBS)),
            dma((2, pairs, DIRECT)), dma((2, pairs, DIRECT)), dma((2, SUBS)), dma((2, SUBS)),
            dma((nd,)), dma((nd,)), dma((nd,)), dma((nd,)),
        ],
        compiler_params=pltpu.CompilerParams(
            collective_id=0, has_side_effects=True, vmem_limit_bytes=24 * 2**20
        ),
        name="exchange",
    )(*(in_hbm(x) for x in (concentration, entry, absorb, taps, measured)))


def descent_kernel(nd, part_ref, later_ref, res_ref, out_hbm, res_hbm, stage, res_stage, sems, res_sem):
    cells, depth, height = part_ref.shape
    width = height // nd
    di = lax.axis_index("depth")
    group = cells // WRITES

    for n in range(WRITES):
        def tile(i, carry):
            rows = pl.ds(pl.multiple_of(i * ROWS, ROWS), ROWS)
            later = later_ref[rows, :]
            for b in range(n * group, (n + 1) * group):
                stage[b, rows, :] = part_ref[b, rows, :] + later
            return carry

        lax.fori_loop(0, depth // ROWS, tile, 0)
        part = pl.ds(n * group, group)
        pltpu.make_async_copy(stage.at[part], out_hbm.at[part], sems.at[n]).start()

    for k in range(nd):
        @pl.when(di == k)
        def _():
            res_stage[...] = res_ref[:, k * width:(k + 1) * width]
    residual = pltpu.make_async_copy(res_stage, res_hbm, res_sem.at[0])
    residual.start()
    for n in range(WRITES):
        part = pl.ds(n * group, group)
        pltpu.make_async_copy(stage.at[part], out_hbm.at[part], sems.at[n]).wait()
    residual.wait()


def write_descent(nd, part, later, residual):
    cells, depth, height = part.shape
    f32 = jnp.float32
    shapes = (part.shape, (cells, height // nd))
    return pl.pallas_call(
        functools.partial(descent_kernel, nd),
        out_shape=[jax.ShapeDtypeStruct(shape, f32) for shape in shapes],
        in_specs=[pl.BlockSpec(memory_space=pltpu.VMEM)] * 3,
        out_specs=[pl.BlockSpec(memory_space=pltpu.HBM)] * 2,
        scratch_shapes=[
            pltpu.VMEM(shapes[0], f32),
            pltpu.VMEM(shapes[1], f32),
            pltpu.SemaphoreType.DMA((WRITES,)),
            pltpu.SemaphoreType.DMA((1,)),
        ],
        compiler_params=pltpu.CompilerParams(vmem_limit_bytes=24 * 2**20),
        name="descent",
    )(part, later, residual)


def solution(mesh):
    nb, nd = mesh.shape["beam"], mesh.shape["depth"]

    def local(concentration, entry_intensity, absorb, blur_taps, measured):
        part, later, residual = exchange(
            nb, nd, concentration, entry_intensity, absorb.reshape(1, -1), blur_taps, measured
        )
        return tuple(write_descent(nd, part, later, residual))

    return jax.shard_map(
        local,
        mesh=mesh,
        in_specs=(P("beam", "depth", None), P("depth", None), P(), P(), P("beam", None)),
        out_specs=(P("beam", "depth", None), P("beam", "depth")),
        check_vma=False,
    )
```

```python
import functools

import jax
import jax.numpy as jnp
from jax import lax
from jax.experimental import pallas as pl
from jax.experimental.pallas import tpu as pltpu
from jax.sharding import PartitionSpec as P

MESH = pl.DeviceIdType.MESH
ROWS, LANES = 8, 128
SUBS = (2, 4)
DIRECT = (0, 2)
WRITES = 8


def blur(x, taps, sign):
    width = x.shape[1]
    lane = lax.broadcasted_iota(jnp.int32, x.shape, 1)
    total = jnp.zeros_like(x)
    for k in range(5):
        step = sign * (k - 2)
        moved = x if step == 0 else pltpu.roll(x, (-step) % width, 1)
        inside = (lane + step >= 0) & (lane + step < width)
        total = total + taps[k] * jnp.where(inside, moved, 0.0)
    return total


def exchange_kernel(
    nb, nd, c_hbm, entry_hbm, absorb_hbm, taps_hbm, measured_hbm,
    part, later_out, res_out,
    w, entry, absorb, taps_ref, measured, light, wide, tot, pbuf, ps, qbuf, dbuf, fs, fbuf, before,
    img, rs, ag,
    load_sem, small_sem, a_send, a_recv, b_send, b_recv, d_send, d_recv, f_send, f_recv,
    rs_send, rs_recv, ag_send, ag_recv,
):
    cells, depth, height = w.shape
    half = depth // 2
    subs = [half // n for n in SUBS]
    relayed = [n - d for n, d in zip(SUBS, DIRECT)]
    pairs = nb // 2
    bi = lax.axis_index("beam")
    di = lax.axis_index("depth")
    core = lax.rem(bi, 2)
    pair = bi // 2
    partner = bi + 1 - 2 * core
    tiles = depth // ROWS
    lane_blocks = height // LANES
    pieces = (cells // ROWS) * lane_blocks
    owners = min(nd, pieces)
    per = pieces // owners

    own_start = pl.multiple_of(core * half, ROWS)
    other_start = pl.multiple_of((1 - core) * half, ROWS)
    own_rows = pl.ds(own_start, half)
    other_rows = pl.ds(other_start, half)

    def at(ph, start, s):
        return pl.ds(pl.multiple_of(start + s * subs[ph], ROWS), subs[ph])

    def piece(ph, s):
        return pl.ds(s * subs[ph], subs[ph])

    loads = []
    for start in (other_start, own_start):
        for s in range(SUBS[0]):
            chunk = at(0, start, s)
            copy = pltpu.make_async_copy(
                c_hbm.at[:, chunk, :], w.at[:, chunk, :], load_sem.at[len(loads)]
            )
            copy.start()
            loads.append(copy)
    small = []
    for source, place in (
        (absorb_hbm, absorb), (entry_hbm, entry), (taps_hbm, taps_ref), (measured_hbm, measured)
    ):
        copy = pltpu.make_async_copy(source, place, small_sem.at[len(small)])
        copy.start()
        small.append(copy)

    barrier = pltpu.get_barrier_semaphore()
    for k in range(1, nb):
        pl.semaphore_signal(
            barrier, inc=1, device_id={"beam": lax.rem(bi + k, nb)}, device_id_type=MESH
        )
    for k in range(1, nd):
        pl.semaphore_signal(
            barrier, inc=1, device_id={"depth": lax.rem(di + k, nd)}, device_id_type=MESH
        )

    def sum_cells(start, s):
        def tile(i, carry):
            rows = pl.ds(pl.multiple_of(start + s * subs[0] + i * ROWS, ROWS), ROWS)
            parts = [w[b, rows, :] for b in range(4)]
            for b in range(4, cells):
                parts[b % 4] = parts[b % 4] + w[b, rows, :]
            tot[0, rows, :] = (parts[0] + parts[1]) + (parts[2] + parts[3])
            return carry

        lax.fori_loop(0, subs[0] // ROWS, tile, 0)

    def sum_weighted(start, s):
        rows = [
            pl.ds(pl.multiple_of(start + s * subs[1] + i * ROWS, ROWS), ROWS)
            for i in range(subs[1] // ROWS)
        ]
        for j in range(lane_blocks):
            lanes = pl.ds(j * LANES, LANES)
            acc = None
            for b in range(cells):
                factor = wide[b, :, lanes]
                terms = [factor * part[b, r, lanes] for r in rows]
                acc = terms if acc is None else [x + y for x, y in zip(acc, terms)]
            for r, x in zip(rows, acc):
                tot[1, r, lanes] = light[r, lanes] * x

    def to_partner(ph, slot):
        return pltpu.make_async_remote_copy(
            src_ref=tot.at[ph, other_rows if slot == 0 else own_rows, :],
            dst_ref=pbuf.at[ph, slot],
            send_sem=a_send.at[ph, slot],
            recv_sem=a_recv.at[ph, slot],
            device_id={"beam": partner},
            device_id_type=MESH,
        )

    def to_pair(ph, target, s):
        return pltpu.make_async_remote_copy(
            src_ref=ps.at[ph, piece(ph, s)],
            dst_ref=qbuf.at[ph, pair, piece(ph, s)],
            send_sem=b_send.at[ph, target, s],
            recv_sem=b_recv.at[ph, pair, s],
            device_id={"beam": 2 * target + core},
            device_id_type=MESH,
        )

    def from_pair(ph, source, s):
        return pltpu.make_async_remote_copy(
            src_ref=ps.at[ph, piece(ph, s)],
            dst_ref=qbuf.at[ph, source, piece(ph, s)],
            send_sem=b_send.at[ph, source, s],
            recv_sem=b_recv.at[ph, source, s],
            device_id={"beam": 2 * source + core},
            device_id_type=MESH,
        )

    def to_cross(ph, target, s):
        return pltpu.make_async_remote_copy(
            src_ref=ps.at[ph, piece(ph, s)],
            dst_ref=dbuf.at[ph, pair, piece(ph, s)],
            send_sem=d_send.at[ph, target, s],
            recv_sem=d_recv.at[ph, pair, s],
            device_id={"beam": 2 * target + 1 - core},
            device_id_type=MESH,
        )

    def from_cross(ph, source, s):
        return pltpu.make_async_remote_copy(
            src_ref=ps.at[ph, piece(ph, s)],
            dst_ref=dbuf.at[ph, source, piece(ph, s)],
            send_sem=d_send.at[ph, source, s],
            recv_sem=d_recv.at[ph, source, s],
            device_id={"beam": 2 * source + 1 - core},
            device_id_type=MESH,
        )

    def forward(ph, s):
        return pltpu.make_async_remote_copy(
            src_ref=fs.at[ph, piece(ph, s)],
            dst_ref=fbuf.at[ph, piece(ph, s)],
            send_sem=f_send.at[ph, s],
            recv_sem=f_recv.at[ph, s],
            device_id={"beam": partner},
            device_id_type=MESH,
        )

    def downstream(ph, other):
        return other > pair if ph == 0 else other < pair

    def upstream(ph, other):
        return other < pair if ph == 0 else other > pair

    def exchange_begin(ph, sums):
        for s in range(SUBS[ph]):
            sums(other_start, s)
        if ph == 0:
            pl.semaphore_wait(barrier, nb - 1 + nd - 1)
        to_partner(ph, 0).start()
        for s in range(SUBS[ph]):
            sums(own_start, s)
            if s == 0:
                to_partner(ph, 0).wait_recv()
            if pairs > 1:
                ps[ph, piece(ph, s)] = tot[ph, at(ph, own_start, s), :] + pbuf[ph, 0, piece(ph, s)]
                for target in range(pairs):
                    @pl.when(downstream(ph, target))
                    def _():
                        to_pair(ph, target, s).start()
                        if s >= relayed[ph]:
                            to_cross(ph, target, s).start()
        to_partner(ph, 1).start()

    def collect(ph, s):
        first = 0 if ph == 0 else pairs - 1
        from_pair(ph, first, s).wait_recv()
        fs[ph, piece(ph, s)] = qbuf[ph, first, piece(ph, s)]
        for source in range(pairs):
            if source != first:
                @pl.when(upstream(ph, source))
                def _():
                    from_pair(ph, source, s).wait_recv()
                    fs[ph, piece(ph, s)] = fs[ph, piece(ph, s)] + qbuf[ph, source, piece(ph, s)]

    def when_upstream(ph, body):
        if pairs > 1:
            pl.when(upstream(ph, 0 if ph == 0 else pairs - 1))(body)

    def relay(ph):
        def body():
            for s in range(relayed[ph]):
                collect(ph, s)
                forward(ph, s).start()

        when_upstream(ph, body)

    def from_core(ph, slot, result):
        takes = core == (1 if ph == 0 else 0)
        rows = own_rows if slot == 0 else other_rows

        @pl.when(takes)
        def _():
            result[rows, :] = pbuf[ph, slot]

        @pl.when(jnp.logical_not(takes))
        def _():
            result[rows, :] = jnp.zeros((half, height), jnp.float32)

    def finish_own(ph, result):
        from_core(ph, 0, result)

        def body():
            for s in range(SUBS[ph]):
                if s >= relayed[ph]:
                    collect(ph, s)
                rows = at(ph, own_start, s)
                result[rows, :] = result[rows, :] + fs[ph, piece(ph, s)]

        when_upstream(ph, body)

    def finish_other(ph, result):
        to_partner(ph, 1).wait_recv()
        from_core(ph, 1, result)

        def body():
            for s in range(SUBS[ph]):
                rows = at(ph, other_start, s)
                if s < relayed[ph]:
                    forward(ph, s).wait_recv()
                    result[rows, :] = result[rows, :] + fbuf[ph, piece(ph, s)]
                else:
                    for source in range(pairs):
                        @pl.when(upstream(ph, source))
                        def _():
                            from_cross(ph, source, s).wait_recv()
                            result[rows, :] = result[rows, :] + dbuf[ph, source, piece(ph, s)]

        when_upstream(ph, body)

    def exchange_sent(ph):
        to_partner(ph, 0).wait_send()
        to_partner(ph, 1).wait_send()
        if pairs > 1:
            for s in range(SUBS[ph]):
                for target in range(pairs):
                    @pl.when(downstream(ph, target))
                    def _():
                        to_pair(ph, target, s).wait_send()
                        if s >= relayed[ph]:
                            to_cross(ph, target, s).wait_send()

            @pl.when(upstream(ph, 0 if ph == 0 else pairs - 1))
            def _():
                for s in range(relayed[ph]):
                    forward(ph, s).wait_send()

    def sum_loaded(start, s):
        loads[s if start is other_start else SUBS[0] + s].wait()
        sum_cells(start, s)

    exchange_begin(0, sum_loaded)
    for copy in small:
        copy.wait()

    def weigh(i, carry):
        rows = pl.ds(pl.multiple_of(i * ROWS, ROWS), ROWS)
        for j in range(lane_blocks):
            lanes = pl.ds(j * LANES, LANES)
            rate = -absorb[:, lanes]
            prior = w[0, rows, lanes]
            part[0, rows, lanes] = prior
            for b in range(1, cells):
                c = w[b, rows, lanes]
                part[b, rows, lanes] = c * jnp.exp(rate * prior)
                prior = prior + c
        return carry

    def emit(g, carry):
        for j in range(lane_blocks):
            lanes = pl.ds(j * LANES, LANES)
            sums = []
            for r in range(ROWS):
                acc = [None, None]
                for t in range(tiles):
                    rows = pl.ds(t * ROWS, ROWS)
                    term = light[rows, lanes] * part[g * ROWS + r, rows, lanes]
                    acc[t % 2] = term if acc[t % 2] is None else acc[t % 2] + term
                sums.append(jnp.sum(acc[0] + acc[1], axis=0, keepdims=True))
            img[g * lane_blocks + j] = jnp.concatenate(sums, axis=0)
        return carry

    lax.fori_loop(0, tiles, weigh, 0)
    relay(0)
    finish_own(0, before)
    finish_other(0, before)
    light[...] = entry[...] * jnp.exp(-absorb[...] * before[...])
    lax.fori_loop(0, cells // ROWS, emit, 0)

    def guarded(index, body):
        if owners == nd:
            body()
        else:
            pl.when(index < owners)(body)

    def scatter(target, k):
        return pltpu.make_async_remote_copy(
            src_ref=img.at[pl.ds(target * per, per)],
            dst_ref=rs.at[di],
            send_sem=rs_send.at[k],
            recv_sem=rs_recv.at[di],
            device_id={"depth": target},
            device_id_type=MESH,
        )

    def scattered(source, k):
        return pltpu.make_async_remote_copy(
            src_ref=img.at[pl.ds(0, per)],
            dst_ref=rs.at[source],
            send_sem=rs_send.at[k],
            recv_sem=rs_recv.at[source],
            device_id={"depth": source},
            device_id_type=MESH,
        )

    def gather(target, k):
        mine = pl.ds(di * per, per)
        return pltpu.make_async_remote_copy(
            src_ref=ag.at[mine],
            dst_ref=ag.at[mine],
            send_sem=ag_send.at[k],
            recv_sem=ag_recv.at[di],
            device_id={"depth": target},
            device_id_type=MESH,
        )

    def gathered(source, k):
        theirs = pl.ds(source * per, per)
        return pltpu.make_async_remote_copy(
            src_ref=ag.at[theirs],
            dst_ref=ag.at[theirs],
            send_sem=ag_send.at[k],
            recv_sem=ag_recv.at[source],
            device_id={"depth": source},
            device_id_type=MESH,
        )

    for k in range(1, nd):
        target = lax.rem(di + k, nd)
        guarded(target, lambda target=target, k=k: scatter(target, k).start())

    def reduce_own():
        total = img[pl.ds(di * per, per)]
        for k in range(1, nd):
            source = lax.rem(di + k, nd)
            scattered(source, k).wait_recv()
            total = total + rs[source]
        ag[pl.ds(di * per, per)] = total * (1.0 / (depth * nd))
        for k in range(1, nd):
            gather(lax.rem(di + k, nd), k).start()

    guarded(di, reduce_own)

    for k in range(1, nd):
        source = lax.rem(di + k, nd)
        guarded(source, lambda source=source, k=k: gathered(source, k).wait_recv())

    image = jnp.concatenate(
        [
            jnp.concatenate([ag[g * lane_blocks + j] for j in range(lane_blocks)], axis=1)
            for g in range(cells // ROWS)
        ],
        axis=0,
    )
    taps = [taps_ref[k] for k in range(5)]
    residual = blur(image, taps, 1) - measured[...]
    res_out[...] = residual
    back = blur(residual, taps, -1)
    for b in range(cells):
        wide[b] = jnp.broadcast_to(back[b:b + 1, :], (ROWS, height))

    exchange_begin(1, sum_weighted)

    def adjoint(i, carry):
        rows = pl.ds(pl.multiple_of(i * ROWS, ROWS), ROWS)
        for j in range(lane_blocks):
            lanes = pl.ds(j * LANES, LANES)
            rate, lamp = absorb[:, lanes], light[rows, lanes]
            prior = None
            q = []
            for b in range(cells):
                scale = lamp * wide[b, :, lanes]
                c = w[b, rows, lanes]
                q.append(scale if b == 0 else scale * jnp.exp(-rate * prior))
                prior = c if b == 0 else prior + c
            later = None
            for b in reversed(range(cells)):
                part[b, rows, lanes] = -q[b] if later is None else rate * later - q[b]
                term = q[b] * w[b, rows, lanes]
                later = term if later is None else later + term
        return carry

    lax.fori_loop(0, tiles, adjoint, 0)
    relay(1)
    finish_own(1, before)
    finish_other(1, before)
    later_out[...] = absorb[...] * before[...]

    exchange_sent(0)
    exchange_sent(1)
    for k in range(1, nd):
        target = lax.rem(di + k, nd)
        guarded(target, lambda target=target, k=k: scatter(target, k).wait_send())

    def sent():
        for k in range(1, nd):
            gather(lax.rem(di + k, nd), k).wait_send()

    guarded(di, sent)


def in_hbm(x):
    return pltpu.with_memory_space_constraint(x, pltpu.HBM)


def exchange(nb, nd, concentration, entry, absorb, taps, measured):
    cells, depth, height = concentration.shape
    half, pairs = depth // 2, nb // 2
    most = max(SUBS)
    pieces = (cells // ROWS) * (height // LANES)
    per = pieces // min(nd, pieces)
    f32 = jnp.float32
    dma = pltpu.SemaphoreType.DMA
    vmem = pl.BlockSpec(memory_space=pltpu.VMEM)
    return pl.pallas_call(
        functools.partial(exchange_kernel, nb, nd),
        out_shape=[
            jax.ShapeDtypeStruct((cells, depth, height), f32),
            jax.ShapeDtypeStruct((depth, height), f32),
            jax.ShapeDtypeStruct((cells, height), f32),
        ],
        in_specs=[pl.BlockSpec(memory_space=pltpu.HBM)] * 5,
        out_specs=[vmem] * 3,
        scratch_shapes=[
            pltpu.VMEM((cells, depth, height), f32),
            pltpu.VMEM((depth, height), f32),
            pltpu.VMEM(absorb.shape, f32),
            pltpu.SMEM(taps.shape, f32),
            pltpu.VMEM((cells, height), f32),
            pltpu.VMEM((depth, height), f32),
            pltpu.VMEM((cells, ROWS, height), f32),
            pltpu.VMEM((2, depth, height), f32),
            pltpu.VMEM((2, 2, half, height), f32),
            pltpu.VMEM((2, half, height), f32),
            pltpu.VMEM((2, pairs, half, height), f32),
            pltpu.VMEM((2, pairs, half, height), f32),
            pltpu.VMEM((2, half, height), f32),
            pltpu.VMEM((2, half, height), f32),
            pltpu.VMEM((depth, height), f32),
            pltpu.VMEM((pieces, ROWS, LANES), f32),
            pltpu.VMEM((nd, per, ROWS, LANES), f32),
            pltpu.VMEM((pieces, ROWS, LANES), f32),
            dma((2 * SUBS[0],)), dma((4,)), dma((2, 2)), dma((2, 2)),
            dma((2, pairs, most)), dma((2, pairs, most)),
            dma((2, pairs, most)), dma((2, pairs, most)), dma((2, most)), dma((2, most)),
            dma((nd,)), dma((nd,)), dma((nd,)), dma((nd,)),
        ],
        compiler_params=pltpu.CompilerParams(
            collective_id=0, has_side_effects=True, vmem_limit_bytes=24 * 2**20
        ),
        name="exchange",
    )(*(in_hbm(x) for x in (concentration, entry, absorb, taps, measured)))


def descent_kernel(nd, part_ref, later_ref, res_ref, out_hbm, res_hbm, stage, res_stage, sems, res_sem):
    cells, depth, height = part_ref.shape
    width = height // nd
    di = lax.axis_index("depth")
    group = cells // WRITES

    for n in range(WRITES):
        def tile(i, carry):
            rows = pl.ds(pl.multiple_of(i * ROWS, ROWS), ROWS)
            later = later_ref[rows, :]
            for b in range(n * group, (n + 1) * group):
                stage[b, rows, :] = part_ref[b, rows, :] + later
            return carry

        lax.fori_loop(0, depth // ROWS, tile, 0)
        part = pl.ds(n * group, group)
        pltpu.make_async_copy(stage.at[part], out_hbm.at[part], sems.at[n]).start()

    for k in range(nd):
        @pl.when(di == k)
        def _():
            res_stage[...] = res_ref[:, k * width:(k + 1) * width]
    residual = pltpu.make_async_copy(res_stage, res_hbm, res_sem.at[0])
    residual.start()
    for n in range(WRITES):
        part = pl.ds(n * group, group)
        pltpu.make_async_copy(stage.at[part], out_hbm.at[part], sems.at[n]).wait()
    residual.wait()


def write_descent(nd, part, later, residual):
    cells, depth, height = part.shape
    f32 = jnp.float32
    shapes = (part.shape, (cells, height // nd))
    return pl.pallas_call(
        functools.partial(descent_kernel, nd),
        out_shape=[jax.ShapeDtypeStruct(shape, f32) for shape in shapes],
        in_specs=[pl.BlockSpec(memory_space=pltpu.VMEM)] * 3,
        out_specs=[pl.BlockSpec(memory_space=pltpu.HBM)] * 2,
        scratch_shapes=[
            pltpu.VMEM(shapes[0], f32),
            pltpu.VMEM(shapes[1], f32),
            pltpu.SemaphoreType.DMA((WRITES,)),
            pltpu.SemaphoreType.DMA((1,)),
        ],
        compiler_params=pltpu.CompilerParams(vmem_limit_bytes=24 * 2**20),
        name="descent",
    )(part, later, residual)


def solution(mesh):
    nb, nd = mesh.shape["beam"], mesh.shape["depth"]

    def local(concentration, entry_intensity, absorb, blur_taps, measured):
        part, later, residual = exchange(
            nb, nd, concentration, entry_intensity, absorb.reshape(1, -1), blur_taps, measured
        )
        return tuple(write_descent(nd, part, later, residual))

    return jax.shard_map(
        local,
        mesh=mesh,
        in_specs=(P("beam", "depth", None), P("depth", None), P(), P(), P("beam", None)),
        out_specs=(P("beam", "depth", None), P("beam", "depth")),
        check_vma=False,
    )
```

```python
import functools

import jax
import jax.numpy as jnp
from jax import lax
from jax.experimental import pallas as pl
from jax.experimental.pallas import tpu as pltpu
from jax.sharding import PartitionSpec as P

MESH = pl.DeviceIdType.MESH
ROWS, LANES = 8, 128
SUBS = (2, 2)
DIRECT = (0, 0)
WRITES = 8


def blur(x, taps, sign):
    width = x.shape[1]
    lane = lax.broadcasted_iota(jnp.int32, x.shape, 1)
    total = jnp.zeros_like(x)
    for k in range(5):
        step = sign * (k - 2)
        moved = x if step == 0 else pltpu.roll(x, (-step) % width, 1)
        inside = (lane + step >= 0) & (lane + step < width)
        total = total + taps[k] * jnp.where(inside, moved, 0.0)
    return total


def exchange_kernel(
    nb, nd, c_hbm, entry_hbm, absorb_hbm, taps_hbm, measured_hbm,
    part, later_out, res_out,
    w, entry, absorb, taps_ref, measured, light, wide, tot, pbuf, ps, qbuf, dbuf, fs, fbuf, before,
    img, rs, ag,
    load_sem, small_sem, a_send, a_recv, b_send, b_recv, d_send, d_recv, f_send, f_recv,
    rs_send, rs_recv, ag_send, ag_recv,
):
    cells, depth, height = w.shape
    half = depth // 2
    subs = [half // n for n in SUBS]
    relayed = [n - d for n, d in zip(SUBS, DIRECT)]
    pairs = nb // 2
    bi = lax.axis_index("beam")
    di = lax.axis_index("depth")
    core = lax.rem(bi, 2)
    pair = bi // 2
    partner = bi + 1 - 2 * core
    tiles = depth // ROWS
    lane_blocks = height // LANES
    pieces = (cells // ROWS) * lane_blocks
    owners = min(nd, pieces)
    per = pieces // owners

    own_start = pl.multiple_of(core * half, ROWS)
    other_start = pl.multiple_of((1 - core) * half, ROWS)
    own_rows = pl.ds(own_start, half)
    other_rows = pl.ds(other_start, half)

    def at(ph, start, s):
        return pl.ds(pl.multiple_of(start + s * subs[ph], ROWS), subs[ph])

    def piece(ph, s):
        return pl.ds(s * subs[ph], subs[ph])

    loads = []
    for start in (other_start, own_start):
        for s in range(SUBS[0]):
            chunk = at(0, start, s)
            copy = pltpu.make_async_copy(
                c_hbm.at[:, chunk, :], w.at[:, chunk, :], load_sem.at[len(loads)]
            )
            copy.start()
            loads.append(copy)
    small = []
    for source, place in (
        (absorb_hbm, absorb), (entry_hbm, entry), (taps_hbm, taps_ref), (measured_hbm, measured)
    ):
        copy = pltpu.make_async_copy(source, place, small_sem.at[len(small)])
        copy.start()
        small.append(copy)

    barrier = pltpu.get_barrier_semaphore()
    for k in range(1, nb):
        pl.semaphore_signal(
            barrier, inc=1, device_id={"beam": lax.rem(bi + k, nb)}, device_id_type=MESH
        )
    for k in range(1, nd):
        pl.semaphore_signal(
            barrier, inc=1, device_id={"depth": lax.rem(di + k, nd)}, device_id_type=MESH
        )

    def sum_cells(start, s):
        def tile(i, carry):
            rows = pl.ds(pl.multiple_of(start + s * subs[0] + i * ROWS, ROWS), ROWS)
            parts = [w[b, rows, :] for b in range(4)]
            for b in range(4, cells):
                parts[b % 4] = parts[b % 4] + w[b, rows, :]
            tot[0, rows, :] = (parts[0] + parts[1]) + (parts[2] + parts[3])
            return carry

        lax.fori_loop(0, subs[0] // ROWS, tile, 0)

    def sum_weighted(start, s):
        rows = [
            pl.ds(pl.multiple_of(start + s * subs[1] + i * ROWS, ROWS), ROWS)
            for i in range(subs[1] // ROWS)
        ]
        for j in range(lane_blocks):
            lanes = pl.ds(j * LANES, LANES)
            acc = None
            for b in range(cells):
                factor = wide[b, :, lanes]
                terms = [factor * part[b, r, lanes] for r in rows]
                acc = terms if acc is None else [x + y for x, y in zip(acc, terms)]
            for r, x in zip(rows, acc):
                tot[1, r, lanes] = light[r, lanes] * x

    def to_partner(ph, slot):
        return pltpu.make_async_remote_copy(
            src_ref=tot.at[ph, other_rows if slot == 0 else own_rows, :],
            dst_ref=pbuf.at[ph, slot],
            send_sem=a_send.at[ph, slot],
            recv_sem=a_recv.at[ph, slot],
            device_id={"beam": partner},
            device_id_type=MESH,
        )

    def to_pair(ph, target, s):
        return pltpu.make_async_remote_copy(
            src_ref=ps.at[ph, piece(ph, s)],
            dst_ref=qbuf.at[ph, pair, piece(ph, s)],
            send_sem=b_send.at[ph, target, s],
            recv_sem=b_recv.at[ph, pair, s],
            device_id={"beam": 2 * target + core},
            device_id_type=MESH,
        )

    def from_pair(ph, source, s):
        return pltpu.make_async_remote_copy(
            src_ref=ps.at[ph, piece(ph, s)],
            dst_ref=qbuf.at[ph, source, piece(ph, s)],
            send_sem=b_send.at[ph, source, s],
            recv_sem=b_recv.at[ph, source, s],
            device_id={"beam": 2 * source + core},
            device_id_type=MESH,
        )

    def to_cross(ph, target, s):
        return pltpu.make_async_remote_copy(
            src_ref=ps.at[ph, piece(ph, s)],
            dst_ref=dbuf.at[ph, pair, piece(ph, s)],
            send_sem=d_send.at[ph, target, s],
            recv_sem=d_recv.at[ph, pair, s],
            device_id={"beam": 2 * target + 1 - core},
            device_id_type=MESH,
        )

    def from_cross(ph, source, s):
        return pltpu.make_async_remote_copy(
            src_ref=ps.at[ph, piece(ph, s)],
            dst_ref=dbuf.at[ph, source, piece(ph, s)],
            send_sem=d_send.at[ph, source, s],
            recv_sem=d_recv.at[ph, source, s],
            device_id={"beam": 2 * source + 1 - core},
            device_id_type=MESH,
        )

    def forward(ph, s):
        return pltpu.make_async_remote_copy(
            src_ref=fs.at[ph, piece(ph, s)],
            dst_ref=fbuf.at[ph, piece(ph, s)],
            send_sem=f_send.at[ph, s],
            recv_sem=f_recv.at[ph, s],
            device_id={"beam": partner},
            device_id_type=MESH,
        )

    def downstream(ph, other):
        return other > pair if ph == 0 else other < pair

    def upstream(ph, other):
        return other < pair if ph == 0 else other > pair

    def exchange_begin(ph, sums):
        for s in range(SUBS[ph]):
            sums(other_start, s)
        if ph == 0:
            pl.semaphore_wait(barrier, nb - 1 + nd - 1)
        to_partner(ph, 0).start()
        for s in range(SUBS[ph]):
            sums(own_start, s)
            if s == 0:
                to_partner(ph, 0).wait_recv()
            if pairs > 1:
                ps[ph, piece(ph, s)] = tot[ph, at(ph, own_start, s), :] + pbuf[ph, 0, piece(ph, s)]
                for target in range(pairs):
                    @pl.when(downstream(ph, target))
                    def _():
                        to_pair(ph, target, s).start()
                        if s >= relayed[ph]:
                            to_cross(ph, target, s).start()
        to_partner(ph, 1).start()

    def collect(ph, s):
        first = 0 if ph == 0 else pairs - 1
        from_pair(ph, first, s).wait_recv()
        fs[ph, piece(ph, s)] = qbuf[ph, first, piece(ph, s)]
        for source in range(pairs):
            if source != first:
                @pl.when(upstream(ph, source))
                def _():
                    from_pair(ph, source, s).wait_recv()
                    fs[ph, piece(ph, s)] = fs[ph, piece(ph, s)] + qbuf[ph, source, piece(ph, s)]

    def when_upstream(ph, body):
        if pairs > 1:
            pl.when(upstream(ph, 0 if ph == 0 else pairs - 1))(body)

    def relay(ph):
        def body():
            for s in range(relayed[ph]):
                collect(ph, s)
                forward(ph, s).start()

        when_upstream(ph, body)

    def from_core(ph, slot, result):
        takes = core == (1 if ph == 0 else 0)
        rows = own_rows if slot == 0 else other_rows

        @pl.when(takes)
        def _():
            result[rows, :] = pbuf[ph, slot]

        @pl.when(jnp.logical_not(takes))
        def _():
            result[rows, :] = jnp.zeros((half, height), jnp.float32)

    def from_cores(ph, result):
        to_partner(ph, 1).wait_recv()
        from_core(ph, 0, result)
        from_core(ph, 1, result)

    def finish_own(ph, result):
        def body():
            for s in range(SUBS[ph]):
                if s >= relayed[ph]:
                    collect(ph, s)
                rows = at(ph, own_start, s)
                result[rows, :] = result[rows, :] + fs[ph, piece(ph, s)]

        when_upstream(ph, body)

    def finish_other(ph, result):
        def body():
            for s in range(SUBS[ph]):
                rows = at(ph, other_start, s)
                if s < relayed[ph]:
                    forward(ph, s).wait_recv()
                    result[rows, :] = result[rows, :] + fbuf[ph, piece(ph, s)]
                else:
                    for source in range(pairs):
                        @pl.when(upstream(ph, source))
                        def _():
                            from_cross(ph, source, s).wait_recv()
                            result[rows, :] = result[rows, :] + dbuf[ph, source, piece(ph, s)]

        when_upstream(ph, body)

    def exchange_sent(ph):
        to_partner(ph, 0).wait_send()
        to_partner(ph, 1).wait_send()
        if pairs > 1:
            for s in range(SUBS[ph]):
                for target in range(pairs):
                    @pl.when(downstream(ph, target))
                    def _():
                        to_pair(ph, target, s).wait_send()
                        if s >= relayed[ph]:
                            to_cross(ph, target, s).wait_send()

            @pl.when(upstream(ph, 0 if ph == 0 else pairs - 1))
            def _():
                for s in range(relayed[ph]):
                    forward(ph, s).wait_send()

    def sum_loaded(start, s):
        loads[s if start is other_start else SUBS[0] + s].wait()
        sum_cells(start, s)

    exchange_begin(0, sum_loaded)
    for copy in small:
        copy.wait()

    def weigh(start, first, last):
        def tile(i, carry):
            rows = pl.ds(pl.multiple_of(start + i * ROWS, ROWS), ROWS)
            for j in range(lane_blocks):
                lanes = pl.ds(j * LANES, LANES)
                rate = -absorb[:, lanes]
                prior = w[0, rows, lanes]
                part[0, rows, lanes] = prior
                for b in range(1, cells):
                    c = w[b, rows, lanes]
                    part[b, rows, lanes] = c * jnp.exp(rate * prior)
                    prior = prior + c
            return carry

        lax.fori_loop(first, last, tile, 0)

    def enter(rows):
        light[rows, :] = entry[rows, :] * jnp.exp(-absorb[...] * before[rows, :])

    def emit(start, last):
        def group(g, carry):
            for j in range(lane_blocks):
                lanes = pl.ds(j * LANES, LANES)
                tile_rows = [
                    pl.ds(pl.multiple_of(start + t * ROWS, ROWS), ROWS)
                    for t in range(half // ROWS)
                ]
                lamps = [light[rows, lanes] for rows in tile_rows]
                sums = []
                for r in range(ROWS):
                    b = g * ROWS + r
                    acc = [wide[b, :, lanes] if last else None, None]
                    for t, rows in enumerate(tile_rows):
                        term = lamps[t] * part[b, rows, lanes]
                        acc[t % 2] = term if acc[t % 2] is None else acc[t % 2] + term
                    total = acc[0] + acc[1]
                    if last:
                        sums.append(jnp.sum(total, axis=0, keepdims=True))
                    else:
                        wide[b, :, lanes] = total
                if last:
                    img[g * lane_blocks + j] = jnp.concatenate(sums, axis=0)
            return carry

        lax.fori_loop(0, cells // ROWS, group, 0)

    half_tiles = half // ROWS
    weigh(own_start, 0, half_tiles)
    weigh(other_start, 0, half_tiles // 2)
    from_cores(0, before)
    relay(0)
    weigh(other_start, half_tiles // 2, half_tiles)
    finish_own(0, before)
    enter(own_rows)
    emit(own_start, False)
    finish_other(0, before)
    enter(other_rows)
    emit(other_start, True)

    def guarded(index, body):
        if owners == nd:
            body()
        else:
            pl.when(index < owners)(body)

    def scatter(target, k):
        return pltpu.make_async_remote_copy(
            src_ref=img.at[pl.ds(target * per, per)],
            dst_ref=rs.at[di],
            send_sem=rs_send.at[k],
            recv_sem=rs_recv.at[di],
            device_id={"depth": target},
            device_id_type=MESH,
        )

    def scattered(source, k):
        return pltpu.make_async_remote_copy(
            src_ref=img.at[pl.ds(0, per)],
            dst_ref=rs.at[source],
            send_sem=rs_send.at[k],
            recv_sem=rs_recv.at[source],
            device_id={"depth": source},
            device_id_type=MESH,
        )

    def gather(target, k):
        mine = pl.ds(di * per, per)
        return pltpu.make_async_remote_copy(
            src_ref=ag.at[mine],
            dst_ref=ag.at[mine],
            send_sem=ag_send.at[k],
            recv_sem=ag_recv.at[di],
            device_id={"depth": target},
            device_id_type=MESH,
        )

    def gathered(source, k):
        theirs = pl.ds(source * per, per)
        return pltpu.make_async_remote_copy(
            src_ref=ag.at[theirs],
            dst_ref=ag.at[theirs],
            send_sem=ag_send.at[k],
            recv_sem=ag_recv.at[source],
            device_id={"depth": source},
            device_id_type=MESH,
        )

    for k in range(1, nd):
        target = lax.rem(di + k, nd)
        guarded(target, lambda target=target, k=k: scatter(target, k).start())

    def reduce_own():
        total = img[pl.ds(di * per, per)]
        for k in range(1, nd):
            source = lax.rem(di + k, nd)
            scattered(source, k).wait_recv()
            total = total + rs[source]
        ag[pl.ds(di * per, per)] = total * (1.0 / (depth * nd))
        for k in range(1, nd):
            gather(lax.rem(di + k, nd), k).start()

    guarded(di, reduce_own)

    for k in range(1, nd):
        source = lax.rem(di + k, nd)
        guarded(source, lambda source=source, k=k: gathered(source, k).wait_recv())

    image = jnp.concatenate(
        [
            jnp.concatenate([ag[g * lane_blocks + j] for j in range(lane_blocks)], axis=1)
            for g in range(cells // ROWS)
        ],
        axis=0,
    )
    taps = [taps_ref[k] for k in range(5)]
    residual = blur(image, taps, 1) - measured[...]
    res_out[...] = residual
    back = blur(residual, taps, -1)
    for b in range(cells):
        wide[b] = jnp.broadcast_to(back[b:b + 1, :], (ROWS, height))

    exchange_begin(1, sum_weighted)

    def adjoint(i, carry):
        rows = pl.ds(pl.multiple_of(i * ROWS, ROWS), ROWS)
        for j in range(lane_blocks):
            lanes = pl.ds(j * LANES, LANES)
            rate, lamp = absorb[:, lanes], light[rows, lanes]
            prior = None
            q = []
            for b in range(cells):
                scale = lamp * wide[b, :, lanes]
                c = w[b, rows, lanes]
                q.append(scale if b == 0 else scale * jnp.exp(-rate * prior))
                prior = c if b == 0 else prior + c
            later = None
            for b in reversed(range(cells)):
                part[b, rows, lanes] = -q[b] if later is None else rate * later - q[b]
                term = q[b] * w[b, rows, lanes]
                later = term if later is None else later + term
        return carry

    lax.fori_loop(0, tiles, adjoint, 0)
    from_cores(1, before)
    relay(1)
    finish_own(1, before)
    later_out[own_rows, :] = absorb[...] * before[own_rows, :]
    finish_other(1, before)
    later_out[other_rows, :] = absorb[...] * before[other_rows, :]

    exchange_sent(0)
    exchange_sent(1)
    for k in range(1, nd):
        target = lax.rem(di + k, nd)
        guarded(target, lambda target=target, k=k: scatter(target, k).wait_send())

    def sent():
        for k in range(1, nd):
            gather(lax.rem(di + k, nd), k).wait_send()

    guarded(di, sent)


def in_hbm(x):
    return pltpu.with_memory_space_constraint(x, pltpu.HBM)


def exchange(nb, nd, concentration, entry, absorb, taps, measured):
    cells, depth, height = concentration.shape
    half, pairs = depth // 2, nb // 2
    most = max(SUBS)
    pieces = (cells // ROWS) * (height // LANES)
    per = pieces // min(nd, pieces)
    f32 = jnp.float32
    dma = pltpu.SemaphoreType.DMA
    vmem = pl.BlockSpec(memory_space=pltpu.VMEM)
    return pl.pallas_call(
        functools.partial(exchange_kernel, nb, nd),
        out_shape=[
            jax.ShapeDtypeStruct((cells, depth, height), f32),
            jax.ShapeDtypeStruct((depth, height), f32),
            jax.ShapeDtypeStruct((cells, height), f32),
        ],
        in_specs=[pl.BlockSpec(memory_space=pltpu.HBM)] * 5,
        out_specs=[vmem] * 3,
        scratch_shapes=[
            pltpu.VMEM((cells, depth, height), f32),
            pltpu.VMEM((depth, height), f32),
            pltpu.VMEM(absorb.shape, f32),
            pltpu.SMEM(taps.shape, f32),
            pltpu.VMEM((cells, height), f32),
            pltpu.VMEM((depth, height), f32),
            pltpu.VMEM((cells, ROWS, height), f32),
            pltpu.VMEM((2, depth, height), f32),
            pltpu.VMEM((2, 2, half, height), f32),
            pltpu.VMEM((2, half, height), f32),
            pltpu.VMEM((2, pairs, half, height), f32),
            pltpu.VMEM((2, pairs, half, height), f32),
            pltpu.VMEM((2, half, height), f32),
            pltpu.VMEM((2, half, height), f32),
            pltpu.VMEM((depth, height), f32),
            pltpu.VMEM((pieces, ROWS, LANES), f32),
            pltpu.VMEM((nd, per, ROWS, LANES), f32),
            pltpu.VMEM((pieces, ROWS, LANES), f32),
            dma((2 * SUBS[0],)), dma((4,)), dma((2, 2)), dma((2, 2)),
            dma((2, pairs, most)), dma((2, pairs, most)),
            dma((2, pairs, most)), dma((2, pairs, most)), dma((2, most)), dma((2, most)),
            dma((nd,)), dma((nd,)), dma((nd,)), dma((nd,)),
        ],
        compiler_params=pltpu.CompilerParams(
            collective_id=0, has_side_effects=True, vmem_limit_bytes=24 * 2**20
        ),
        name="exchange",
    )(*(in_hbm(x) for x in (concentration, entry, absorb, taps, measured)))


def descent_kernel(nd, part_ref, later_ref, res_ref, out_hbm, res_hbm, stage, res_stage, sems, res_sem):
    cells, depth, height = part_ref.shape
    width = height // nd
    di = lax.axis_index("depth")
    group = cells // WRITES

    for n in range(WRITES):
        def tile(i, carry):
            rows = pl.ds(pl.multiple_of(i * ROWS, ROWS), ROWS)
            later = later_ref[rows, :]
            for b in range(n * group, (n + 1) * group):
                stage[b, rows, :] = part_ref[b, rows, :] + later
            return carry

        lax.fori_loop(0, depth // ROWS, tile, 0)
        part = pl.ds(n * group, group)
        pltpu.make_async_copy(stage.at[part], out_hbm.at[part], sems.at[n]).start()

    for k in range(nd):
        @pl.when(di == k)
        def _():
            res_stage[...] = res_ref[:, k * width:(k + 1) * width]
    residual = pltpu.make_async_copy(res_stage, res_hbm, res_sem.at[0])
    residual.start()
    for n in range(WRITES):
        part = pl.ds(n * group, group)
        pltpu.make_async_copy(stage.at[part], out_hbm.at[part], sems.at[n]).wait()
    residual.wait()


def write_descent(nd, part, later, residual):
    cells, depth, height = part.shape
    f32 = jnp.float32
    shapes = (part.shape, (cells, height // nd))
    return pl.pallas_call(
        functools.partial(descent_kernel, nd),
        out_shape=[jax.ShapeDtypeStruct(shape, f32) for shape in shapes],
        in_specs=[pl.BlockSpec(memory_space=pltpu.VMEM)] * 3,
        out_specs=[pl.BlockSpec(memory_space=pltpu.HBM)] * 2,
        scratch_shapes=[
            pltpu.VMEM(shapes[0], f32),
            pltpu.VMEM(shapes[1], f32),
            pltpu.SemaphoreType.DMA((WRITES,)),
            pltpu.SemaphoreType.DMA((1,)),
        ],
        compiler_params=pltpu.CompilerParams(vmem_limit_bytes=24 * 2**20),
        name="descent",
    )(part, later, residual)


def solution(mesh):
    nb, nd = mesh.shape["beam"], mesh.shape["depth"]

    def local(concentration, entry_intensity, absorb, blur_taps, measured):
        part, later, residual = exchange(
            nb, nd, concentration, entry_intensity, absorb.reshape(1, -1), blur_taps, measured
        )
        return tuple(write_descent(nd, part, later, residual))

    return jax.shard_map(
        local,
        mesh=mesh,
        in_specs=(P("beam", "depth", None), P("depth", None), P(), P(), P("beam", None)),
        out_specs=(P("beam", "depth", None), P("beam", "depth")),
        check_vma=False,
    )
```
